128 devices in a mesh: head: 8 (over z_lo, y), resp: 16 (over z_hi, x, core).
Axes of the slice: x: 4, y: 4, z: 4 (z_hi: 2, z_lo: 2; z = z_hi * 2 + z_lo), core: 2. Of those that a mesh axis runs over, the one named last changes fastest.
Arguments:
- queries: bfloat16 [16, 128, 64, 128], P('resp', None, 'head'), may hold values from -8 to 8
- resp_keys: bfloat16 [16, 128, 8, 128], P('resp', None, 'head'), may hold values from -6 to 6
- resp_values: bfloat16 [16, 128, 8, 128], P('resp', None, 'head'), may hold values from -6 to 6
- out_grad: bfloat16 [16, 128, 64, 128], P('resp', None, 'head'), may hold values from -6 to 6
- prefix_keys: bfloat16 [8192, 8, 128], P('resp', 'head'), may hold values from -4 to 4
- prefix_values: bfloat16 [8192, 8, 128], P('resp', 'head'), may hold values from -6 to 6
- w_query: bfloat16 [5120, 8192], P(None, 'head'), may hold values from -0.0625 to 0.0625
- w_key: bfloat16 [5120, 1024], P(None, 'head'), may hold values from -0.1875 to 0.1875
- w_value: bfloat16 [5120, 1024], P(None, 'head'), may hold values from -0.1875 to 0.1875
- resp_lengths: int32 [16], replicated, may hold values from 1 to 128, 1280 in all
Outputs:
- d_hidden: bfloat16 [16, 128, 5120], P('resp', 'head')
- prefix_dk: bfloat16 [8192, 8, 128], P('resp', 'head')
- prefix_dv: bfloat16 [8192, 8, 128], P('resp', 'head')
The draws below stay inside these ranges and needn't reach their ends.
Inputs may be any that keep to these rules, and one draw needn't show every extreme that they name: `resp_lengths`: some response has all 128 rows live.
All inputs are finite; a program needn't handle non-finite values.
Results may differ from the reference program's by a relative error of at most 0.019.
Values may be sent and summed in bfloat16 or wider, within the bound.
A program may use at most 128 MiB of HBM per device.

```python
import math
import jax
import jax.numpy as jnp
import numpy as np
from jax import lax

D = 5120
H = 64
KVH = 8
DH = 128
R_LEN = 128
RESPONSES = 16
P_SIZE = 8192
N_HEAD = 8


def draw_prefix_keys(key, part):
    key = jax.random.fold_in(key, 11)
    base = jnp.clip(jax.random.normal(key, (P_SIZE, KVH, DH), jnp.float32), -4.0, 4.0)
    return base.astype(jnp.bfloat16)


def draw_queries(key, part):
    key = jax.random.fold_in(key, 12)
    base = jnp.clip(jax.random.normal(key, (RESPONSES, R_LEN, H, DH), jnp.float32), -6.0, 6.0)
    return base.astype(jnp.bfloat16)


def levels(key, extent, split, smallest, top_value):
    def one(dim, shards_of):
        steps = jax.random.uniform(jax.random.fold_in(jax.random.fold_in(key, 6), dim), (shards_of,), jnp.float32, smallest / len(split), top_value / len(split))
        return jnp.repeat(jnp.exp(steps), extent[dim] // shards_of).reshape((-1,) + (1,) * (len(extent) - dim - 1))

    factor_of = one(*split[0])
    for cut in split[1:]:
        factor_of = factor_of * one(*cut)
    return factor_of


def profile(amount, total, most, skew):
    weights = [(1 << 20) // math.isqrt(standing ** skew) + 1 for standing in range(2, amount + 1)]
    spare, given = total - most - (amount - 1), [1] * (amount - 1)
    while spare > 0:
        free = [i for i in range(amount - 1) if given[i] < most]
        mass, left = sum([weights[i] for i in free]), spare
        for i in free:
            more = min(most - given[i], max(1, left * weights[i] // mass), spare)
            given[i] = given[i] + more
            spare = spare - more
    return np.array([most] + given)


def ragged(key, count, total, bound, skew):
    if count == 2:
        one = jax.random.randint(key, (), max(1, total - bound), min(bound, total - 1) + 1)
        return jnp.stack([one, total - one])
    sizes = jnp.asarray(profile(count, total, bound, skew), jnp.int32)
    pairs = (count - 1) // 2
    donor, taker = sizes[1:1 + 2 * pairs:2], sizes[2:2 + 2 * pairs:2]
    margin = jnp.minimum(donor - 1, bound - taker)
    shifted = jax.random.randint(jax.random.fold_in(key, 1), (pairs,), 0, 1 << 20) % (margin + 1)
    sizes = sizes.at[1:1 + 2 * pairs:2].set(donor - shifted).at[2:2 + 2 * pairs:2].set(taker + shifted)
    return sizes[jax.random.permutation(jax.random.fold_in(key, 2), count)]


def gaussian(own_key, shape, width, reach, shards=(), held_as=jnp.bfloat16):
    values = jax.random.normal(own_key, shape, jnp.float32) * width
    if len(shards) > 0:
        values = levels(own_key, shape, shards, -0.22, 0.18) * values
    return jnp.clip(values, min=-reach, max=reach).astype(held_as)


def setup_inputs(seed: int = 0) -> dict:
    keys = jax.random.split(jax.random.key(seed), 11)
    queries = draw_queries(jax.random.fold_in(keys[10], 71), 0)
    resp_keys = gaussian(keys[1], (RESPONSES, R_LEN, KVH, DH), 1.0, 6.0, ((0, 16), (2, 8)))
    resp_values = gaussian(keys[2], (RESPONSES, R_LEN, KVH, DH), 1.0, 6.0, ((0, 16), (2, 8)))
    out_grad = gaussian(keys[3], (RESPONSES, R_LEN, H, DH), 1.0, 6.0, ((0, 16), (2, 8)))
    prefix_keys = draw_prefix_keys(jax.random.fold_in(keys[10], 71), 0)
    prefix_values = gaussian(keys[5], (P_SIZE, KVH, DH), 1.0, 6.0, ((0, 16), (1, 8)))
    w_query = gaussian(keys[6], (D, H * DH), (H * DH) ** -0.5, 0.0625, ((1, 8),))
    w_key = gaussian(keys[7], (D, KVH * DH), (KVH * DH) ** -0.5, 0.1875, ((1, 8),))
    w_value = gaussian(keys[8], (D, KVH * DH), (KVH * DH) ** -0.5, 0.1875, ((1, 8),))
    resp_lengths = ragged(keys[9], RESPONSES, RESPONSES * R_LEN * 5 // 8, R_LEN, 2).astype(jnp.int32)
    return dict(queries=queries, resp_keys=resp_keys, resp_values=resp_values, out_grad=out_grad, prefix_keys=prefix_keys, prefix_values=prefix_values, w_query=w_query, w_key=w_key, w_value=w_value, resp_lengths=resp_lengths)


NEG = -1e30


def round_keep(value):
    return lax.optimization_barrier(value.astype(jnp.bfloat16)).astype(jnp.float32)


def head_grads(query_rows, key_rows, value_rows, grad_rows, live_length):
    row_count = query_rows.shape[0]
    scaling = DH ** -0.5
    query_f = query_rows.astype(jnp.float32)
    key_f = key_rows.astype(jnp.float32)
    value_f = value_rows.astype(jnp.float32)
    is_live = jnp.arange(row_count, dtype=jnp.int32) < live_length
    grad_f = jnp.where(is_live[:, None, None], grad_rows, jnp.zeros_like(grad_rows)).astype(jnp.float32)
    scores = jnp.einsum('rgd,kd->grk', query_f, key_f) * scaling
    key_place = jnp.arange(P_SIZE + row_count, dtype=jnp.int32) - P_SIZE
    allowed = key_place[None, :] <= jnp.arange(row_count, dtype=jnp.int32)[:, None]
    scores = jnp.where(allowed[None], scores, NEG)
    highest = jnp.max(scores, -1, keepdims=True)
    log_total = highest + jnp.log(jnp.sum(jnp.exp(scores - highest), -1, keepdims=True))
    attend = jnp.exp(scores - log_total)
    attend_b = round_keep(attend)
    pulled = jnp.einsum('rgd,kd->grk', grad_f, value_f)
    row_delta = jnp.sum(attend_b * pulled, -1, keepdims=True)
    slope = round_keep(attend * (pulled - row_delta))
    query_grad = jnp.einsum('grk,kd->rgd', slope, key_f) * scaling
    key_grad = jnp.einsum('grk,rgd->kd', slope, query_f) * scaling
    value_grad = jnp.einsum('grk,rgd->kd', attend_b, grad_f)
    return query_grad, key_grad, value_grad


def reference(queries, resp_keys, resp_values, out_grad, prefix_keys, prefix_values, w_query, w_key, w_value, resp_lengths):
    group_size = H // KVH

    def one_response(folded, element):
        query_b, key_b, value_b, grad_b, live_length = element

        def one_head(head_id):
            keys_all = jnp.concatenate([lax.dynamic_index_in_dim(prefix_keys, head_id, 1, keepdims=False), lax.dynamic_index_in_dim(key_b, head_id, 1, keepdims=False)], 0)
            values_all = jnp.concatenate([lax.dynamic_index_in_dim(prefix_values, head_id, 1, keepdims=False), lax.dynamic_index_in_dim(value_b, head_id, 1, keepdims=False)], 0)
            query_rows = lax.dynamic_slice_in_dim(query_b, head_id * group_size, group_size, 1)
            grad_rows = lax.dynamic_slice_in_dim(grad_b, head_id * group_size, group_size, 1)
            return head_grads(query_rows, keys_all, values_all, grad_rows, live_length)

        query_grad, key_grad, value_grad = lax.map(one_head, jnp.arange(KVH, dtype=jnp.int32))
        summed_k = folded[0] + key_grad[:, :P_SIZE]
        summed_v = folded[1] + value_grad[:, :P_SIZE]
        query_out = query_grad.transpose(1, 0, 2, 3).reshape(R_LEN, H * DH).astype(jnp.bfloat16)
        key_out = key_grad[:, P_SIZE:].transpose(1, 0, 2).reshape(R_LEN, KVH * DH).astype(jnp.bfloat16)
        value_out = value_grad[:, P_SIZE:].transpose(1, 0, 2).reshape(R_LEN, KVH * DH).astype(jnp.bfloat16)
        return (summed_k, summed_v), (query_out, key_out, value_out)

    start_grads = (jnp.zeros((KVH, P_SIZE, DH), jnp.float32), jnp.zeros((KVH, P_SIZE, DH), jnp.float32))
    (summed_k, summed_v), (query_all, key_all, value_all) = lax.scan(one_response, start_grads, (queries, resp_keys, resp_values, out_grad, resp_lengths))
    query_flat = query_all.reshape(RESPONSES * R_LEN, H * DH)
    key_flat = key_all.reshape(RESPONSES * R_LEN, KVH * DH)
    value_flat = value_all.reshape(RESPONSES * R_LEN, KVH * DH)
    query_cols = H * DH // N_HEAD
    key_cols = KVH * DH // N_HEAD

    def one_group(running, group_id):
        partial_value = jnp.dot(lax.dynamic_slice_in_dim(query_flat, group_id * query_cols, query_cols, 1), lax.dynamic_slice_in_dim(w_query, group_id * query_cols, query_cols, 1).T, preferred_element_type=jnp.float32)
        partial_value = partial_value + jnp.dot(lax.dynamic_slice_in_dim(key_flat, group_id * key_cols, key_cols, 1), lax.dynamic_slice_in_dim(w_key, group_id * key_cols, key_cols, 1).T, preferred_element_type=jnp.float32)
        partial_value = partial_value + jnp.dot(lax.dynamic_slice_in_dim(value_flat, group_id * key_cols, key_cols, 1), lax.dynamic_slice_in_dim(w_value, group_id * key_cols, key_cols, 1).T, preferred_element_type=jnp.float32)
        return running + round_keep(partial_value), None

    summed_hidden, _ = lax.scan(one_group, jnp.zeros((RESPONSES * R_LEN, D), jnp.float32), jnp.arange(N_HEAD, dtype=jnp.int32))
    d_hidden = summed_hidden.reshape(RESPONSES, R_LEN, D).astype(jnp.bfloat16)
    prefix_dk = summed_k.transpose(1, 0, 2).astype(jnp.bfloat16)
    prefix_dv = summed_v.transpose(1, 0, 2).astype(jnp.bfloat16)
    return (d_hidden, prefix_dk, prefix_dv)
```

```python
import functools
import math

import jax
import jax.numpy as jnp
from jax import lax
from jax.experimental import pallas as pl
from jax.experimental.pallas import tpu as pltpu
from jax.sharding import PartitionSpec as P

MESH = pl.DeviceIdType.MESH
NT = (((1,), (1,)), ((), ()))
F32, BF16 = jnp.float32, jnp.bfloat16
PLACES = ((0, 0), (0, 1), (0, 3), (1, 0), (0, 2), (1, 1), (1, 3), (1, 2))
BACK = (0, 2, 1, 3, 4, 6, 5, 7)
BLOCKS = 8
SHARE = 512
CHUNK = 512
SLOTS = 4


def kernel(
    lengths, q_hbm, g_hbm, rk_hbm, rv_hbm, k_hbm, v_hbm, wq_hbm, wk_hbm, wv_hbm,
    hidden_out, dk_out, dv_out,
    q_all, g_all, k_all, v_all, q_scaled, k_turned, prob, grad, top, total, mean,
    log_total, delta, rk, rv, causal_p, causal_d, causal_stat, stat_own, stat_in,
    dq_turned, dq_in, dq_rows, flat, weight, hid, hid_in, own, dk_in, dv_in,
    local_sem, weight_sem, q_send, q_recv, k_send, k_recv, v_send, v_recv,
    stat_send, stat_recv, dq_send, dq_recv, dk_send, dk_recv, dv_send, dv_recv, hid_send, hid_recv,
):
    rows = q_all.shape[1]
    self_rows = rk.shape[0]
    group = rows // self_rows
    head = lax.axis_index("head")
    resp = lax.axis_index("resp")
    z_lo, y = head // 4, head % 4
    z_hi, x, core = resp // 8, (resp // 2) % 4, resp % 2
    scaling = q_all.shape[2] ** -0.5
    log2e = math.log2(math.e)
    chunks = hid.shape[1] // CHUNK

    def class_mate(n):
        dz, dx = PLACES[n]
        return (head, ((z_hi + dz) % 2) * 8 + ((x + dx) % 4) * 2 + core)

    sibling = (head, z_hi * 8 + x * 2 + (1 - core))

    def head_index(e):
        return ((z_lo + e // 4) % 2) * 4 + (y + e % 4) % 4

    def local(i, source, target):
        return pltpu.make_async_copy(source, target, local_sem.at[i])

    loads = [
        local(0, k_hbm, k_all.at[pl.ds(0, SHARE), :]),
        local(1, v_hbm, v_all.at[pl.ds(0, SHARE), :]),
        local(2, q_hbm, q_all.at[0]),
        local(3, g_hbm, g_all.at[0]),
        local(4, rk_hbm, rk),
        local(5, rv_hbm, rv),
    ]
    for load in loads:
        load.start()

    def weight_loads(c, slot):
        piece = pl.ds(pl.multiple_of(c * CHUNK, CHUNK), CHUNK)
        wide = q_all.shape[2]
        width = group * wide
        return [
            pltpu.make_async_copy(wq_hbm.at[piece, :], weight.at[slot, :, pl.ds(0, width)], weight_sem.at[slot, 0]),
            pltpu.make_async_copy(wk_hbm.at[piece, :], weight.at[slot, :, pl.ds(width, wide)], weight_sem.at[slot, 1]),
            pltpu.make_async_copy(
                wv_hbm.at[piece, :], weight.at[slot, :, pl.ds(width + wide, wide)], weight_sem.at[slot, 2]
            ),
        ]

    barrier = pltpu.get_barrier_semaphore()
    partners = [class_mate(n) for n in range(1, BLOCKS)] + [sibling] + [(head_index(e), resp) for e in range(1, 8)]
    for partner in partners:
        pl.semaphore_signal(barrier, inc=1, device_id=partner, device_id_type=MESH)

    for load in loads:
        load.wait()
    place = lax.broadcasted_iota(jnp.int32, (rows, 1), 0)
    live = place < lengths[resp] * group
    g_all[0] = jnp.where(live, g_all[0], jnp.zeros_like(g_all[0]))

    pl.semaphore_wait(barrier, len(partners))

    def remote(source, target, send, recv, device):
        return pltpu.make_async_remote_copy(
            src_ref=source, dst_ref=target, send_sem=send, recv_sem=recv, device_id=device, device_id_type=MESH
        )

    pair = [
        remote(q_all.at[0], q_all.at[1], q_send.at[0], q_recv.at[0], sibling),
        remote(g_all.at[0], g_all.at[1], q_send.at[1], q_recv.at[1], sibling),
    ]
    for copy in pair:
        copy.start()

    def block(n):
        return pl.ds(pl.multiple_of(n * SHARE, SHARE), SHARE)

    shares = []
    for n in range(1, BLOCKS):
        there = pl.ds(BACK[n] * SHARE, SHARE)
        here = pl.ds(0, SHARE)
        for held, send, recv in ((k_all, k_send, k_recv), (v_all, v_send, v_recv)):
            copy = remote(held.at[here, :], held.at[there, :], send.at[n], recv.at[BACK[n]], class_mate(n))
            copy.start()
            shares.append(copy)
    for c in range(SLOTS):
        for load in weight_loads(c, c):
            load.start()

    def scale_queries(slot):
        exact = q_all[slot].astype(F32) * (scaling * log2e)
        high = exact.astype(BF16)
        q_scaled[slot, :, : q_all.shape[2]] = high
        q_scaled[slot, :, q_all.shape[2] :] = (exact - high.astype(F32)).astype(BF16)

    def first_pass(keys, values, slot, allowed):
        twice = jnp.concatenate([keys, keys], axis=1)
        scores = lax.dot_general(twice, q_scaled[slot], NT, preferred_element_type=F32)
        if allowed is not None:
            scores = jnp.where(allowed, scores, -1e30)
        pulled = lax.dot_general(values, g_all[slot], NT, preferred_element_type=F32)
        high = jnp.max(scores, axis=0, keepdims=True)
        weights = jnp.exp2(scores - high)
        amount = jnp.sum(weights, axis=0, keepdims=True)
        centre = jnp.sum(weights * pulled, axis=0, keepdims=True) / amount
        return weights.astype(BF16), (pulled - centre).astype(BF16), high, amount, centre

    scale_queries(0)
    key_place = lax.broadcasted_iota(jnp.int32, (self_rows, rows), 0)
    row_place = lax.broadcasted_iota(jnp.int32, (self_rows, rows), 1) // group
    causal_p[...], causal_d[...], high, amount, centre = first_pass(rk[...], rv[...], 0, key_place <= row_place)
    causal_stat[0], causal_stat[1], causal_stat[2] = high, amount, centre
    for copy in pair:
        copy.wait_recv()
    scale_queries(1)

    def score_block(n, carry):
        here = block(n)

        @pl.when(n > 0)
        def _():
            for held, send, recv in ((k_all, k_send, k_recv), (v_all, v_send, v_recv)):
                remote(held.at[here, :], held.at[here, :], send.at[n], recv.at[n], sibling).wait_recv()

        keys, values = k_all[here, :], v_all[here, :]
        k_turned[:, here] = keys.T
        for slot in range(2):
            mine = pl.ds(slot * rows, rows)
            prob[here, mine], grad[here, mine], high, amount, centre = first_pass(keys, values, slot, None)
            top[n, :, mine] = high
            total[n, :, mine] = amount
            mean[n, :, mine] = centre
        return carry

    lax.fori_loop(0, BLOCKS, score_block, 0)

    for slot in range(2):
        mine = pl.ds(slot * rows, rows)
        high = top[0, :, mine]
        for n in range(1, BLOCKS):
            high = jnp.maximum(high, top[n, :, mine])
        if slot == 0:
            high = jnp.maximum(high, causal_stat[0])
        amount = jnp.zeros_like(high)
        pulled = jnp.zeros_like(high)
        for n in range(BLOCKS):
            part = total[n, :, mine] * jnp.exp2(top[n, :, mine] - high)
            amount += part
            pulled += part * mean[n, :, mine]
        if slot == 0:
            part = causal_stat[1] * jnp.exp2(causal_stat[0] - high)
            amount += part
            pulled += part * causal_stat[2]
        stat_own[slot, 0:1] = high
        stat_own[slot, 1:2] = amount
        stat_own[slot, 2:3] = pulled
        stat_own[slot, 3:8] = jnp.zeros((5, rows), F32)
    stats = [
        remote(stat_own.at[slot], stat_in.at[1 - slot], stat_send.at[slot], stat_recv.at[1 - slot], sibling)
        for slot in range(2)
    ]
    for copy in stats:
        copy.start()
    for copy in stats:
        copy.wait()
    for slot in range(2):
        mine = pl.ds(slot * rows, rows)
        high = jnp.maximum(stat_own[slot, 0:1], stat_in[slot, 0:1])
        left = jnp.exp2(stat_own[slot, 0:1] - high)
        right = jnp.exp2(stat_in[slot, 0:1] - high)
        amount = stat_own[slot, 1:2] * left + stat_in[slot, 1:2] * right
        log_total[:, mine] = high + jnp.log2(amount)
        delta[:, mine] = (stat_own[slot, 2:3] * left + stat_in[slot, 2:3] * right) / amount

    def second_pass(weights, pulled, high, centre, mine):
        attend = weights.astype(F32) * jnp.exp2(high - log_total[:, mine])
        slope = attend * (pulled.astype(F32) + (centre - delta[:, mine]))
        return attend.astype(BF16), slope.astype(BF16)

    for copy in shares:
        copy.wait_send()

    def to_owner(n, back, device):
        here = block(n)
        return [
            remote(k_all.at[here, :], dk_in.at[back], dk_send.at[n], dk_recv.at[back], device),
            remote(v_all.at[here, :], dv_in.at[back], dv_send.at[n], dv_recv.at[back], device),
        ]

    q_flat = q_all[...].reshape(2 * rows, q_all.shape[2])
    g_flat = g_all[...].reshape(2 * rows, q_all.shape[2])

    def gradient_block(n):
        here = block(n)
        parts = []
        for slot in range(2):
            mine = pl.ds(slot * rows, rows)
            attend, slope = second_pass(prob[here, mine], grad[here, mine], top[n, :, mine], mean[n, :, mine], mine)
            grad[here, mine] = slope
            parts.append((attend, slope))
        attend = jnp.concatenate([parts[0][0], parts[1][0]], axis=1)
        slope = jnp.concatenate([parts[0][1], parts[1][1]], axis=1)
        dv = jnp.dot(attend, g_flat, preferred_element_type=F32)
        dk = jnp.dot(slope, q_flat, preferred_element_type=F32) * scaling
        return dk, dv

    def gradient_step(u, carry):
        n = (u + 1) % BLOCKS
        here = block(n)
        dk, dv = gradient_block(n)

        @pl.when(n > 0)
        def _():
            k_all[here, :] = dk.astype(BF16)
            v_all[here, :] = dv.astype(BF16)

        @pl.when(n == 0)
        def _():
            own[0] = dk
            own[1] = dv

        for place in range(1, BLOCKS):

            @pl.when(n == place)
            def _():
                for copy in to_owner(place, BACK[place], class_mate(place)):
                    copy.start()

        return carry

    lax.fori_loop(0, BLOCKS, gradient_step, 0)

    columns = 256

    def turned_slot(slot):
        def part(i, carry):
            there = pl.ds(pl.multiple_of(slot * rows + i * columns, columns), columns)
            dq_turned[:, there] = jnp.dot(k_turned[...], grad[:, there], preferred_element_type=F32)
            return carry

        lax.fori_loop(0, rows // columns, part, 0)

    turned_slot(1)
    give_dq = remote(dq_turned.at[:, pl.ds(rows, rows)], dq_in, dq_send.at[0], dq_recv.at[0], sibling)
    give_dq.start()
    turned_slot(0)
    mine = pl.ds(0, rows)
    attend, slope = second_pass(causal_p[...], causal_d[...], causal_stat[0], causal_stat[2], mine)
    wide = q_all.shape[2]
    flat[:, group * wide : (group + 1) * wide] = (
        jnp.dot(slope, q_all[0], preferred_element_type=F32) * scaling
    ).astype(BF16)
    flat[:, (group + 1) * wide :] = jnp.dot(attend, g_all[0], preferred_element_type=F32).astype(BF16)
    self_part = jnp.dot(rk[...].T, slope, preferred_element_type=F32)
    give_dq.wait_recv()
    dq_rows[...] = ((dq_turned[:, mine] + self_part + dq_in[...]) * scaling).T
    for i in range(group):
        flat[:, i * wide : (i + 1) * wide] = dq_rows[pl.ds(i, self_rows, stride=group), :].astype(BF16)

    share_rows = hidden_out.shape[0]

    def hidden_copy(c, e):
        there = head_index(e)
        back = (e // 4) * 4 + (4 - e % 4) % 4
        piece = pl.ds(pl.multiple_of(c * CHUNK, CHUNK), CHUNK)
        return remote(
            hid.at[pl.ds(pl.multiple_of(there * share_rows, share_rows), share_rows), piece],
            hid_in.at[back, :, piece],
            hid_send.at[c, e],
            hid_recv.at[c, back],
            (there, resp),
        )

    def hidden_chunk(c, carry):
        slot = c % SLOTS
        for load in weight_loads(c, slot):
            load.wait()
        turned = lax.dot_general(weight[slot], flat[...], NT, preferred_element_type=F32)
        piece = pl.ds(pl.multiple_of(c * CHUNK, CHUNK), CHUNK)
        hid[:, piece] = turned.T.astype(BF16)
        for e in range(1, 8):
            hidden_copy(c, e).start()

        @pl.when(c + SLOTS < chunks)
        def _():
            for load in weight_loads(c + SLOTS, slot):
                load.start()

        return carry

    lax.fori_loop(0, chunks, hidden_chunk, 0)

    dk, dv = own[0], own[1]
    for n in range(1, BLOCKS):
        back = BACK[n]
        for copy in to_owner(back, n, class_mate(back)):
            copy.wait_recv()
        dk = dk + dk_in[n].astype(F32)
        dv = dv + dv_in[n].astype(F32)
    dk_out[...] = dk.astype(BF16)
    dv_out[...] = dv.astype(BF16)

    def hidden_wait(c, carry):
        for e in range(1, 8):
            hidden_copy(c, e).wait()
        return carry

    lax.fori_loop(0, chunks, hidden_wait, 0)
    result = hid[pl.ds(pl.multiple_of(head * share_rows, share_rows), share_rows), :].astype(F32)
    for e in range(1, 8):
        result = result + hid_in[e].astype(F32)
    hidden_out[...] = result.astype(BF16)

    for n in range(1, BLOCKS):
        for copy in to_owner(n, BACK[n], class_mate(n)):
            copy.wait_send()
    for copy in pair + [give_dq]:
        copy.wait_send()


def per_device(
    queries, resp_keys, resp_values, out_grad, prefix_keys, prefix_values, w_query, w_key, w_value, resp_lengths
):
    self_rows, group, size = queries.shape[1:]
    rows = self_rows * group
    width = w_query.shape[0]
    heads = 8
    keys = BLOCKS * SHARE
    chunks = width // CHUNK
    vmem, dma = pltpu.VMEM, pltpu.SemaphoreType.DMA
    whole = pl.BlockSpec(memory_space=pltpu.VMEM)
    hidden, dk, dv = pl.pallas_call(
        kernel,
        out_shape=(
            jax.ShapeDtypeStruct((self_rows // heads, width), BF16),
            jax.ShapeDtypeStruct((SHARE, size), BF16),
            jax.ShapeDtypeStruct((SHARE, size), BF16),
        ),
        in_specs=[pl.BlockSpec(memory_space=pltpu.SMEM)] + [pl.BlockSpec(memory_space=pl.ANY)] * 9,
        out_specs=(whole, whole, whole),
        scratch_shapes=[
            vmem((2, rows, size), BF16),
            vmem((2, rows, size), BF16),
            vmem((keys, size), BF16),
            vmem((keys, size), BF16),
            vmem((2, rows, 2 * size), BF16),
            vmem((size, keys), BF16),
            vmem((keys, 2 * rows), BF16),
            vmem((keys, 2 * rows), BF16),
            vmem((BLOCKS, 1, 2 * rows), F32),
            vmem((BLOCKS, 1, 2 * rows), F32),
            vmem((BLOCKS, 1, 2 * rows), F32),
            vmem((1, 2 * rows), F32),
            vmem((1, 2 * rows), F32),
            vmem((self_rows, size), BF16),
            vmem((self_rows, size), BF16),
            vmem((self_rows, rows), BF16),
            vmem((self_rows, rows), BF16),
            vmem((3, 1, rows), F32),
            vmem((2, 8, rows), F32),
            vmem((2, 8, rows), F32),
            vmem((size, 2 * rows), F32),
            vmem((size, rows), F32),
            vmem((rows, size), F32),
            vmem((self_rows, (group + 2) * size), BF16),
            vmem((SLOTS, CHUNK, (group + 2) * size), BF16),
            vmem((self_rows, width), BF16),
            vmem((heads, self_rows // heads, width), BF16),
            vmem((2, SHARE, size), F32),
            vmem((BLOCKS, SHARE, size), BF16),
            vmem((BLOCKS, SHARE, size), BF16),
            dma((6,)),
            dma((SLOTS, 3)),
            dma((2,)),
            dma((2,)),
            dma((BLOCKS,)),
            dma((BLOCKS,)),
            dma((BLOCKS,)),
            dma((BLOCKS,)),
            dma((2,)),
            dma((2,)),
            dma((1,)),
            dma((1,)),
            dma((BLOCKS,)),
            dma((BLOCKS,)),
            dma((BLOCKS,)),
            dma((BLOCKS,)),
            dma((chunks, 8)),
            dma((chunks, 8)),
        ],
        compiler_params=pltpu.CompilerParams(
            collective_id=0, has_side_effects=True, vmem_limit_bytes=63 * 1024 * 1024
        ),
    )(
        resp_lengths,
        queries.reshape(rows, size),
        out_grad.reshape(rows, size),
        resp_keys.reshape(self_rows, size),
        resp_values.reshape(self_rows, size),
        prefix_keys.reshape(SHARE, size),
        prefix_values.reshape(SHARE, size),
        w_query,
        w_key,
        w_value,
    )
    return hidden[None], dk[:, None], dv[:, None]


def solution(mesh):
    in_specs = (
        P("resp", None, "head", None),
        P("resp", None, "head", None),
        P("resp", None, "head", None),
        P("resp", None, "head", None),
        P("resp", "head", None),
        P("resp", "head", None),
        P(None, "head"),
        P(None, "head"),
        P(None, "head"),
        P(),
    )
    out_specs = (P("resp", "head", None), P("resp", "head", None), P("resp", "head", None))
    return jax.shard_map(
        per_device, mesh=mesh, in_specs=in_specs, out_specs=out_specs, check_vma=False
    )
```

```python
import math

import jax
import jax.numpy as jnp
from jax import lax
from jax.experimental import pallas as pl
from jax.experimental.pallas import tpu as pltpu
from jax.sharding import PartitionSpec as P

MESH = pl.DeviceIdType.MESH
NT = (((1,), (1,)), ((), ()))
F32, BF16 = jnp.float32, jnp.bfloat16
PLACES = (0, 1, 3, 2)
BACK = (0, 2, 1, 3)
BLOCKS = 4
RESPS = 4
SHARE = 512
CHUNK = 512
SLOTS = 4


def kernel(
    lengths, q_hbm, g_hbm, rk_hbm, rv_hbm, k_hbm, v_hbm, wq_hbm, wk_hbm, wv_hbm,
    hidden_out, dk_out, dv_out,
    q_all, g_all, k_all, v_all, q_scaled, k_turned, prob, grad, top, total, mean,
    log_total, delta, rk, rv, causal_p, causal_d, causal_stat, stat_own, stat_in,
    dq_own, dq_give, dq_in, dq_far, dq_far_in, dq_rows, flat, weight, hid, hid_in, dk_sum, dv_sum, dk_in, dv_in,
    local_sem, weight_sem, q_send, q_recv, far_send, far_recv, relay_send, relay_recv, k_send, k_recv, v_send, v_recv,
    stat_send, stat_recv, dq_send, dq_recv, dk_send, dk_recv, dv_send, dv_recv, hid_send, hid_recv,
):
    rows, wide = q_all.shape[1:]
    self_rows = rk.shape[0]
    group = rows // self_rows
    half = rows // 2
    head = lax.axis_index("head")
    resp = lax.axis_index("resp")
    z_lo, y = head // 4, head % 4
    z_hi, x, core = resp // 8, (resp // 2) % 4, resp % 2
    scaling = wide ** -0.5
    log2e = math.log2(math.e)
    chunks = hid.shape[1] // CHUNK

    def along_x(n):
        return (head, z_hi * 8 + ((x + PLACES[n]) % 4) * 2 + core)

    def holder(slot):
        z_there = (z_hi + slot // 2) % 2
        core_there = (core + slot % 2) % 2
        return (head, z_there * 8 + x * 2 + core_there)

    def head_index(e):
        return ((z_lo + e // 4) % 2) * 4 + (y + e % 4) % 4

    loads = [
        pltpu.make_async_copy(source, target, local_sem.at[i])
        for i, (source, target) in enumerate(
            (
                (k_hbm, k_all.at[pl.ds(0, SHARE), :]),
                (v_hbm, v_all.at[pl.ds(0, SHARE), :]),
                (q_hbm, q_all.at[0]),
                (g_hbm, g_all.at[0]),
                (rk_hbm, rk),
                (rv_hbm, rv),
            )
        )
    ]
    for load in loads:
        load.start()

    def weight_loads(c, slot):
        piece = pl.ds(pl.multiple_of(c * CHUNK, CHUNK), CHUNK)
        width = group * wide
        return [
            pltpu.make_async_copy(wq_hbm.at[piece, :], weight.at[slot, :, pl.ds(0, width)], weight_sem.at[slot, 0]),
            pltpu.make_async_copy(wk_hbm.at[piece, :], weight.at[slot, :, pl.ds(width, wide)], weight_sem.at[slot, 1]),
            pltpu.make_async_copy(
                wv_hbm.at[piece, :], weight.at[slot, :, pl.ds(width + wide, wide)], weight_sem.at[slot, 2]
            ),
        ]

    barrier = pltpu.get_barrier_semaphore()
    partners = [along_x(n) for n in range(1, BLOCKS)] + [holder(s) for s in range(1, RESPS)]
    partners += [(head_index(e), resp) for e in range(1, 8)]
    for partner in partners:
        pl.semaphore_signal(barrier, inc=1, device_id=partner, device_id_type=MESH)

    for load in loads:
        load.wait()
    place = lax.broadcasted_iota(jnp.int32, (rows, 1), 0)
    live = place < lengths[resp] * group
    g_all[0] = jnp.where(live, g_all[0], jnp.zeros_like(g_all[0]))

    pl.semaphore_wait(barrier, len(partners))

    def remote(source, target, send, recv, device):
        return pltpu.make_async_remote_copy(
            src_ref=source, dst_ref=target, send_sem=send, recv_sem=recv, device_id=device, device_id_type=MESH
        )

    def block(n):
        return pl.ds(pl.multiple_of(n * SHARE, SHARE), SHARE)

    def halves(part, origin, target, send, recv, device):
        piece = pl.ds(part * half, half)
        return [
            remote(q_all.at[origin, piece, :], q_all.at[target, piece, :], send.at[part, 0], recv.at[part, 0], device),
            remote(g_all.at[origin, piece, :], g_all.at[target, piece, :], send.at[part, 1], recv.at[part, 1], device),
        ]

    far = [halves(part, 0, 2, far_send, far_recv, holder(2)) for part in range(2)]
    for copy in far[0]:
        copy.start()
    pair = [
        remote(q_all.at[0], q_all.at[1], q_send.at[0], q_recv.at[0], holder(1)),
        remote(g_all.at[0], g_all.at[1], q_send.at[1], q_recv.at[1], holder(1)),
    ]
    for copy in pair:
        copy.start()
    shares = []
    for n in range(1, BLOCKS):
        there, here = pl.ds(BACK[n] * SHARE, SHARE), pl.ds(0, SHARE)
        for held, send, recv in ((k_all, k_send, k_recv), (v_all, v_send, v_recv)):
            copy = remote(held.at[here, :], held.at[there, :], send.at[n], recv.at[BACK[n]], along_x(n))
            copy.start()
            shares.append(copy)
    for copy in far[1]:
        copy.start()
    for c in range(SLOTS):
        for load in weight_loads(c, c):
            load.start()

    def scale_queries(slot, start, size):
        piece = pl.ds(start, size)
        exact = q_all[slot, piece, :].astype(F32) * (scaling * log2e)
        high = exact.astype(BF16)
        q_scaled[slot, piece, :wide] = high
        q_scaled[slot, piece, wide:] = (exact - high.astype(F32)).astype(BF16)

    def first_pass(keys, values, slot, start, size, allowed):
        piece = pl.ds(start, size)
        twice = jnp.concatenate([keys, keys], axis=1)
        scores = lax.dot_general(twice, q_scaled[slot, piece, :], NT, preferred_element_type=F32)
        if allowed is not None:
            scores = jnp.where(allowed, scores, -1e30)
        pulled = lax.dot_general(values, g_all[slot, piece, :], NT, preferred_element_type=F32)
        high = jnp.max(scores, axis=0, keepdims=True)
        weights = jnp.exp2(scores - high)
        amount = jnp.sum(weights, axis=0, keepdims=True)
        centre = jnp.sum(weights * pulled, axis=0, keepdims=True) / amount
        return weights.astype(BF16), (pulled - centre).astype(BF16), high, amount, centre

    def score_block(n, parts):
        here = block(n)
        keys, values = k_all[here, :], v_all[here, :]
        for slot, start, size in parts:
            mine = pl.ds(slot * rows + start, size)
            prob[here, mine], grad[here, mine], high, amount, centre = first_pass(keys, values, slot, start, size, None)
            top[n, :, mine] = high
            total[n, :, mine] = amount
            mean[n, :, mine] = centre

    def take_share(n):
        here = block(n)
        for held, send, recv in ((k_all, k_send, k_recv), (v_all, v_send, v_recv)):
            remote(held.at[here, :], held.at[here, :], send.at[n], recv.at[n], holder(1)).wait_recv()

    def turn_keys(n):
        here = block(n)
        k_turned[:, here] = k_all[here, :].T

    relays = [halves(part, 2, 3, relay_send, relay_recv, holder(1)) for part in range(2)]

    def pass_on(part):
        for copy in far[part]:
            copy.wait_recv()
        for copy in relays[part]:
            copy.start()

    def take_relay(part):
        scale_queries(2, part * half, half)
        for copy in relays[part]:
            copy.wait_recv()
        scale_queries(3, part * half, half)

    near = ((0, 0, rows), (1, 0, rows))

    scale_queries(0, 0, rows)
    key_place = lax.broadcasted_iota(jnp.int32, (self_rows, rows), 0)
    row_place = lax.broadcasted_iota(jnp.int32, (self_rows, rows), 1) // group
    causal_p[...], causal_d[...], high, amount, centre = first_pass(
        rk[...], rv[...], 0, 0, rows, key_place <= row_place
    )
    causal_stat[0], causal_stat[1], causal_stat[2] = high, amount, centre
    for copy in pair:
        copy.wait_recv()
    scale_queries(1, 0, rows)

    def near_step(n, carry):
        @pl.when(n > 0)
        def _():
            take_share(n)

        @pl.when(n == 2)
        def _():
            pass_on(0)

        turn_keys(n)
        score_block(n, near)
        return carry

    lax.fori_loop(0, BLOCKS - 1, near_step, 0)
    take_relay(0)

    def far_step(part):
        def step(n, carry):
            score_block(n, ((2, part * half, half), (3, part * half, half)))
            return carry

        return step

    lax.fori_loop(0, BLOCKS - 1, far_step(0), 0)
    take_share(BLOCKS - 1)
    pass_on(1)
    turn_keys(BLOCKS - 1)
    score_block(BLOCKS - 1, near)
    far_step(0)(BLOCKS - 1, 0)
    take_relay(1)
    lax.fori_loop(0, BLOCKS, far_step(1), 0)

    for slot in range(RESPS):
        mine = pl.ds(slot * rows, rows)
        high = top[0, :, mine]
        for n in range(1, BLOCKS):
            high = jnp.maximum(high, top[n, :, mine])
        if slot == 0:
            high = jnp.maximum(high, causal_stat[0])
        amount = jnp.zeros_like(high)
        pulled = jnp.zeros_like(high)
        for n in range(BLOCKS):
            part = total[n, :, mine] * jnp.exp2(top[n, :, mine] - high)
            amount += part
            pulled += part * mean[n, :, mine]
        if slot == 0:
            part = causal_stat[1] * jnp.exp2(causal_stat[0] - high)
            amount += part
            pulled += part * causal_stat[2]
        stat_own[slot : slot + 1] = high + jnp.log2(amount)
        stat_own[RESPS + slot : RESPS + slot + 1] = pulled / amount
    stats = [
        remote(stat_own, stat_in.at[s], stat_send.at[s], stat_recv.at[s], holder(s)) for s in range(1, RESPS)
    ]
    for copy in stats:
        copy.start()
    dk_sum[...] = jnp.zeros_like(dk_sum)
    dv_sum[...] = jnp.zeros_like(dv_sum)
    for copy in stats:
        copy.wait()
    for slot in range(RESPS):
        mine = pl.ds(slot * rows, rows)
        logs = [stat_own[slot : slot + 1]]
        means = [stat_own[RESPS + slot : RESPS + slot + 1]]
        for s in range(1, RESPS):
            there = slot ^ s
            logs.append(stat_in[s, there : there + 1])
            means.append(stat_in[s, RESPS + there : RESPS + there + 1])
        high = jnp.maximum(jnp.maximum(logs[0], logs[1]), jnp.maximum(logs[2], logs[3]))
        parts = [jnp.exp2(value - high) for value in logs]
        amount = parts[0] + parts[1] + parts[2] + parts[3]
        pulled = parts[0] * means[0] + parts[1] * means[1] + parts[2] * means[2] + parts[3] * means[3]
        log_total[:, mine] = high + jnp.log2(amount)
        delta[:, mine] = pulled / amount

    def second_pass(weights, pulled, high, centre, mine):
        attend = weights.astype(F32) * jnp.exp2(high - log_total[:, mine])
        slope = attend * (pulled.astype(F32) + (centre - delta[:, mine]))
        return attend.astype(BF16), slope.astype(BF16)

    def gradient_slot(slot):
        mine = pl.ds(slot * rows, rows)
        for n in range(BLOCKS):
            here = pl.ds(n * SHARE, SHARE)
            attend, slope = second_pass(prob[here, mine], grad[here, mine], top[n, :, mine], mean[n, :, mine], mine)
            prob[here, mine] = attend
            grad[here, mine] = slope
        dv_sum[...] += jnp.dot(prob[:, mine], g_all[slot], preferred_element_type=F32)
        dk_sum[...] += jnp.dot(grad[:, mine], q_all[slot], preferred_element_type=F32)
        return jnp.dot(k_turned[...], grad[:, mine], preferred_element_type=F32)

    dq_give[0] = gradient_slot(3)
    give_far = remote(dq_give.at[0], dq_in.at[0], dq_send.at[0], dq_recv.at[0], holder(1))
    give_far.start()
    far_part = gradient_slot(2)
    give_far.wait_recv()
    dq_far[...] = (far_part + dq_in[0]).astype(BF16)
    give_back = remote(dq_far, dq_far_in, dq_send.at[2], dq_recv.at[2], holder(2))
    give_back.start()
    dq_give[1] = gradient_slot(1)
    give_near = remote(dq_give.at[1], dq_in.at[1], dq_send.at[1], dq_recv.at[1], holder(1))
    give_near.start()

    attend, slope = second_pass(
        causal_p[...], causal_d[...], causal_stat[0], causal_stat[2], pl.ds(0, rows)
    )
    flat[:, group * wide : (group + 1) * wide] = (
        jnp.dot(slope, q_all[0], preferred_element_type=F32) * scaling
    ).astype(BF16)
    flat[:, (group + 1) * wide :] = jnp.dot(attend, g_all[0], preferred_element_type=F32).astype(BF16)
    dq_own[...] = jnp.dot(rk[...].T, slope, preferred_element_type=F32)
    dq_own[...] += gradient_slot(0)

    for copy in shares:
        copy.wait_send()
    k_all[...] = (dk_sum[...] * scaling).astype(BF16)
    v_all[...] = dv_sum[...].astype(BF16)

    def to_owner(n):
        back, here, device = BACK[n], pl.ds(n * SHARE, SHARE), along_x(n)
        return [
            remote(k_all.at[here, :], dk_in.at[back], dk_send.at[n], dk_recv.at[back], device),
            remote(v_all.at[here, :], dv_in.at[back], dv_send.at[n], dv_recv.at[back], device),
        ]

    owed = [copy for n in range(1, BLOCKS) for copy in to_owner(n)]
    for copy in owed:
        copy.start()

    give_near.wait_recv()
    give_back.wait_recv()
    dq_rows[...] = ((dq_own[...] + dq_in[1] + dq_far_in[...].astype(F32)) * scaling).T
    for i in range(group):
        flat[:, i * wide : (i + 1) * wide] = dq_rows[pl.ds(i, self_rows, stride=group), :].astype(BF16)

    share_rows = hidden_out.shape[0]

    def hidden_copy(c, e):
        there = head_index(e)
        back = (e // 4) * 4 + (4 - e % 4) % 4
        piece = pl.ds(pl.multiple_of(c * CHUNK, CHUNK), CHUNK)
        return remote(
            hid.at[pl.ds(pl.multiple_of(there * share_rows, share_rows), share_rows), piece],
            hid_in.at[back, :, piece],
            hid_send.at[c, e],
            hid_recv.at[c, back],
            (there, resp),
        )

    def hidden_chunk(c, carry):
        slot = c % SLOTS
        for load in weight_loads(c, slot):
            load.wait()
        turned = lax.dot_general(weight[slot], flat[...], NT, preferred_element_type=F32)
        piece = pl.ds(pl.multiple_of(c * CHUNK, CHUNK), CHUNK)
        hid[:, piece] = turned.T.astype(BF16)
        for e in range(1, 8):
            hidden_copy(c, e).start()

        @pl.when(c + SLOTS < chunks)
        def _():
            for load in weight_loads(c + SLOTS, slot):
                load.start()

        return carry

    lax.fori_loop(0, chunks, hidden_chunk, 0)

    for copy in owed:
        copy.wait_recv()
    dk = dk_sum[pl.ds(0, SHARE), :] * scaling
    dv = dv_sum[pl.ds(0, SHARE), :]
    for n in range(1, BLOCKS):
        dk = dk + dk_in[n].astype(F32)
        dv = dv + dv_in[n].astype(F32)
    dk_out[...] = dk.astype(BF16)
    dv_out[...] = dv.astype(BF16)

    def hidden_wait(c, carry):
        for e in range(1, 8):
            hidden_copy(c, e).wait()
        return carry

    lax.fori_loop(0, chunks, hidden_wait, 0)
    result = hid[pl.ds(pl.multiple_of(head * share_rows, share_rows), share_rows), :].astype(F32)
    for e in range(1, 8):
        result = result + hid_in[e].astype(F32)
    hidden_out[...] = result.astype(BF16)

    for copy in pair + far[0] + far[1] + relays[0] + relays[1] + [give_far, give_near, give_back] + owed:
        copy.wait_send()


def per_device(
    queries, resp_keys, resp_values, out_grad, prefix_keys, prefix_values, w_query, w_key, w_value, resp_lengths
):
    self_rows, group, size = queries.shape[1:]
    rows = self_rows * group
    width = w_query.shape[0]
    heads = 8
    keys = BLOCKS * SHARE
    chunks = width // CHUNK
    vmem, dma = pltpu.VMEM, pltpu.SemaphoreType.DMA
    whole = pl.BlockSpec(memory_space=pltpu.VMEM)
    hidden, dk, dv = pl.pallas_call(
        kernel,
        out_shape=(
            jax.ShapeDtypeStruct((self_rows // heads, width), BF16),
            jax.ShapeDtypeStruct((SHARE, size), BF16),
            jax.ShapeDtypeStruct((SHARE, size), BF16),
        ),
        in_specs=[pl.BlockSpec(memory_space=pltpu.SMEM)] + [pl.BlockSpec(memory_space=pl.ANY)] * 9,
        out_specs=(whole, whole, whole),
        scratch_shapes=[
            vmem((RESPS, rows, size), BF16),
            vmem((RESPS, rows, size), BF16),
            vmem((keys, size), BF16),
            vmem((keys, size), BF16),
            vmem((RESPS, rows, 2 * size), BF16),
            vmem((size, keys), BF16),
            vmem((keys, RESPS * rows), BF16),
            vmem((keys, RESPS * rows), BF16),
            vmem((BLOCKS, 1, RESPS * rows), F32),
            vmem((BLOCKS, 1, RESPS * rows), F32),
            vmem((BLOCKS, 1, RESPS * rows), F32),
            vmem((1, RESPS * rows), F32),
            vmem((1, RESPS * rows), F32),
            vmem((self_rows, size), BF16),
            vmem((self_rows, size), BF16),
            vmem((self_rows, rows), BF16),
            vmem((self_rows, rows), BF16),
            vmem((3, 1, rows), F32),
            vmem((2 * RESPS, rows), F32),
            vmem((RESPS, 2 * RESPS, rows), F32),
            vmem((size, rows), F32),
            vmem((2, size, rows), F32),
            vmem((2, size, rows), F32),
            vmem((size, rows), BF16),
            vmem((size, rows), BF16),
            vmem((rows, size), F32),
            vmem((self_rows, (group + 2) * size), BF16),
            vmem((SLOTS, CHUNK, (group + 2) * size), BF16),
            vmem((self_rows, width), BF16),
            vmem((heads, self_rows // heads, width), BF16),
            vmem((keys, size), F32),
            vmem((keys, size), F32),
            vmem((BLOCKS, SHARE, size), BF16),
            vmem((BLOCKS, SHARE, size), BF16),
            dma((6,)),
            dma((SLOTS, 3)),
            dma((2,)),
            dma((2,)),
            dma((2, 2)),
            dma((2, 2)),
            dma((2, 2)),
            dma((2, 2)),
            dma((BLOCKS,)),
            dma((BLOCKS,)),
            dma((BLOCKS,)),
            dma((BLOCKS,)),
            dma((RESPS,)),
            dma((RESPS,)),
            dma((3,)),
            dma((3,)),
            dma((BLOCKS,)),
            dma((BLOCKS,)),
            dma((BLOCKS,)),
            dma((BLOCKS,)),
            dma((chunks, 8)),
            dma((chunks, 8)),
        ],
        compiler_params=pltpu.CompilerParams(
            collective_id=0, has_side_effects=True, vmem_limit_bytes=63 * 1024 * 1024
        ),
    )(
        resp_lengths,
        queries.reshape(rows, size),
        out_grad.reshape(rows, size),
        resp_keys.reshape(self_rows, size),
        resp_values.reshape(self_rows, size),
        prefix_keys.reshape(SHARE, size),
        prefix_values.reshape(SHARE, size),
        w_query,
        w_key,
        w_value,
    )
    return hidden[None], dk[:, None], dv[:, None]


def solution(mesh):
    in_specs = (
        P("resp", None, "head", None),
        P("resp", None, "head", None),
        P("resp", None, "head", None),
        P("resp", None, "head", None),
        P("resp", "head", None),
        P("resp", "head", None),
        P(None, "head"),
        P(None, "head"),
        P(None, "head"),
        P(),
    )
    out_specs = (P("resp", "head", None), P("resp", "head", None), P("resp", "head", None))
    return jax.shard_map(
        per_device, mesh=mesh, in_specs=in_specs, out_specs=out_specs, check_vma=False
    )
```

```python
import math

import jax
import jax.numpy as jnp
from jax import lax
from jax.experimental import pallas as pl
from jax.experimental.pallas import tpu as pltpu
from jax.sharding import PartitionSpec as P

MESH = pl.DeviceIdType.MESH
NT = (((1,), (1,)), ((), ()))
F32, BF16 = jnp.float32, jnp.bfloat16
PLACES = (0, 1, 3, 2)
BACK = (0, 2, 1, 3)
BLOCKS = 4
RESPS = 4
HEADS = 8
SHARE = 512
CHUNK = 512
RING = 4


def kernel(
    lengths, q_hbm, g_hbm, rk_hbm, rv_hbm, k_hbm, v_hbm, wq_hbm, wk_hbm, wv_hbm,
    hidden_out, dk_out, dv_out,
    q_all, g_all, k_all, v_all, q_scaled, k_turned, prob, grad, top, total, mean,
    log_total, delta, rk, rv, causal_p, causal_d, causal_stat, stat_own, stat_in,
    dq_self, dq_part, dq_in, dq_far, dq_far_in, dq_rows, self_flat, flat, weight, hid_in,
    dk_sum, dv_sum, dk_in, dv_in,
    local_sem, weight_sem, q_send, q_recv, far_send, far_recv, relay_send, relay_recv, k_send, k_recv, v_send, v_recv,
    stat_send, stat_recv, dq_send, dq_recv, dq_far_send, dq_far_recv, dk_send, dk_recv, dv_send, dv_recv,
    hid_send, hid_recv,
):
    pair_rows, wide = q_all.shape[2:]
    half = pair_rows // 2
    self_rows = rk.shape[0]
    group = 2 * half // self_rows
    head = lax.axis_index("head")
    resp = lax.axis_index("resp")
    z_lo, y = head // 4, head % 4
    z_hi, x, core = resp // 8, (resp // 2) % 4, resp % 2
    scaling = wide ** -0.5
    log2e = math.log2(math.e)
    steps = hid_in.shape[2]
    narrow = CHUNK // 2

    def along_x(n):
        return (head, z_hi * 8 + ((x + PLACES[n]) % 4) * 2 + core)

    def holder(slot):
        z_there = (z_hi + slot // 2) % 2
        core_there = (core + slot % 2) % 2
        return (head, z_there * 8 + x * 2 + core_there)

    def head_index(e):
        return ((z_lo + e // 4) % 2) * 4 + (y + e % 4) % 4

    def first(h, held):
        return held.at[h, 0, pl.ds(0, half), :]

    loads = [
        pltpu.make_async_copy(source, target, local_sem.at[i])
        for i, (source, target) in enumerate(
            (
                (k_hbm, k_all.at[pl.ds(0, SHARE), :]),
                (v_hbm, v_all.at[pl.ds(0, SHARE), :]),
                (rk_hbm, rk),
                (rv_hbm, rv),
            )
        )
    ]
    piece_rows = half // HEADS
    for h in range(2):
        for o in range(HEADS):
            for i, (source, held) in enumerate(((q_hbm, q_all), (g_hbm, g_all))):
                loads.append(
                    pltpu.make_async_copy(
                        source.at[pl.ds((2 * o + h) * piece_rows, piece_rows), :],
                        held.at[h, 0, pl.ds(o * piece_rows, piece_rows), :],
                        local_sem.at[4 + (h * HEADS + o) * 2 + i],
                    )
                )
    for load in loads:
        load.start()

    def weight_loads(v):
        slot, width = v % RING, group * wide
        piece = pl.ds(pl.multiple_of(((v // 2) % steps + (v % 2) * steps) * CHUNK, CHUNK), CHUNK)
        return [
            pltpu.make_async_copy(
                source.at[piece, :], weight.at[slot, :, pl.ds(start, size)], weight_sem.at[slot, j]
            )
            for j, (source, start, size) in enumerate(
                ((wq_hbm, 0, width), (wk_hbm, width, wide), (wv_hbm, width + wide, wide))
            )
        ]

    barrier = pltpu.get_barrier_semaphore()
    partners = [along_x(n) for n in range(1, BLOCKS)] + [holder(s) for s in range(1, RESPS)]
    partners += [(head_index(e), resp) for e in range(1, HEADS)]
    for partner in partners:
        pl.semaphore_signal(barrier, inc=1, device_id=partner, device_id_type=MESH)

    def row_of(h, count):
        return (count >> 6) * 16 + 8 * h + ((count & 63) >> 3)

    for load in loads:
        load.wait()
    for h in range(2):
        place = lax.broadcasted_iota(jnp.int32, (half, 1), 0)
        live = row_of(h, place) < lengths[resp]
        g_all[h, 0, :half] = jnp.where(live, g_all[h, 0, :half], jnp.zeros((half, wide), BF16))

    pl.semaphore_wait(barrier, len(partners))

    def remote(source, target, send, recv, device):
        return pltpu.make_async_remote_copy(
            src_ref=source, dst_ref=target, send_sem=send, recv_sem=recv, device_id=device, device_id_type=MESH
        )

    def block(n):
        return pl.ds(pl.multiple_of(n * SHARE, SHARE), SHARE)

    def rows_to(h, origin, target, send, recv, device):
        (pair, at), (pair_there, at_there) = origin, target
        return [
            remote(
                held.at[h, pair, pl.ds(at * half, half), :],
                held.at[h, pair_there, pl.ds(at_there * half, half), :],
                send.at[h, i],
                recv.at[h, i],
                device,
            )
            for i, held in enumerate((q_all, g_all))
        ]

    far = [rows_to(h, (0, 0), (1, 0), far_send, far_recv, holder(2)) for h in range(2)]
    near = [rows_to(h, (0, 0), (0, 1), q_send, q_recv, holder(1)) for h in range(2)]
    relays = [rows_to(h, (1, 0), (1, 1), relay_send, relay_recv, holder(1)) for h in range(2)]
    for copy in far[0] + near[0] + near[1]:
        copy.start()
    shares = []
    for n in range(1, BLOCKS):
        there, here = pl.ds(BACK[n] * SHARE, SHARE), pl.ds(0, SHARE)
        for held, send, recv in ((k_all, k_send, k_recv), (v_all, v_send, v_recv)):
            copy = remote(held.at[here, :], held.at[there, :], send.at[n], recv.at[BACK[n]], along_x(n))
            copy.start()
            shares.append(copy)
    for copy in far[1]:
        copy.start()
    for v in range(RING):
        for load in weight_loads(v):
            load.start()

    def scale_queries(h, pair, at):
        piece = pl.ds(at * half, half)
        exact = q_all[h, pair, piece, :].astype(F32) * (scaling * log2e)
        high = exact.astype(BF16)
        here = pl.ds((2 * h + pair) * pair_rows + at * half, half)
        q_scaled[here, :wide] = high
        q_scaled[here, wide:] = (exact - high.astype(F32)).astype(BF16)

    def first_pass(keys, values, scaled, pulls, allowed):
        twice = jnp.concatenate([keys, keys], axis=1)
        scores = lax.dot_general(twice, scaled, NT, preferred_element_type=F32)
        if allowed is not None:
            scores = jnp.where(allowed, scores, -1e30)
        pulled = lax.dot_general(values, pulls, NT, preferred_element_type=F32)
        high = jnp.max(scores, axis=0, keepdims=True)
        weights = jnp.exp2(scores - high)
        amount = jnp.sum(weights, axis=0, keepdims=True)
        centre = jnp.sum(weights * pulled, axis=0, keepdims=True) / amount
        return weights.astype(BF16), (pulled - centre).astype(BF16), high, amount, centre

    def pair_columns(h, pair):
        return pl.ds(pl.multiple_of((2 * h + pair) * pair_rows, pair_rows), pair_rows)

    def slot_columns(h, slot):
        return pl.ds((RESPS * h + slot) * half, half)

    def score(n, h, pair):
        here, mine = block(n), pair_columns(h, pair)
        prob[here, mine], grad[here, mine], high, amount, centre = first_pass(
            k_all[here, :], v_all[here, :], q_scaled[mine, :], g_all[h, pair], None
        )
        top[n, :, mine] = high
        total[n, :, mine] = amount
        mean[n, :, mine] = centre

    def take_share(n):
        here = block(n)
        for held, send, recv in ((k_all, k_send, k_recv), (v_all, v_send, v_recv)):
            remote(held.at[here, :], held.at[here, :], send.at[n], recv.at[n], holder(1)).wait_recv()

    def turn_keys(n):
        here = block(n)
        k_turned[:, here] = k_all[here, :].T

    def pass_on(h):
        for copy in far[h]:
            copy.wait_recv()
        for copy in relays[h]:
            copy.start()

    def take_relay(h):
        scale_queries(h, 1, 0)
        for copy in relays[h]:
            copy.wait_recv()
        scale_queries(h, 1, 1)

    for h in range(2):
        scale_queries(h, 0, 0)
        key_place = lax.broadcasted_iota(jnp.int32, (self_rows, half), 0)
        row_place = row_of(h, lax.broadcasted_iota(jnp.int32, (self_rows, half), 1))
        causal_p[h], causal_d[h], high, amount, centre = first_pass(
            rk[...], rv[...], q_scaled[pl.ds(2 * h * pair_rows, half), :], g_all[h, 0, :half], key_place <= row_place
        )
        causal_stat[h, 0], causal_stat[h, 1], causal_stat[h, 2] = high, amount, centre
    for copy in near[0] + near[1]:
        copy.wait_recv()
    scale_queries(0, 0, 1)
    scale_queries(1, 0, 1)

    def near_step(n, carry):
        @pl.when(n > 0)
        def _():
            take_share(n)

        @pl.when(n == 2)
        def _():
            pass_on(0)

        turn_keys(n)
        score(n, 0, 0)
        score(n, 1, 0)
        return carry

    def local_stats(h):
        for slot in range(RESPS):
            mine = slot_columns(h, slot)
            high = top[0, :, mine]
            for n in range(1, BLOCKS):
                high = jnp.maximum(high, top[n, :, mine])
            if slot == 0:
                high = jnp.maximum(high, causal_stat[h, 0])
            amount = jnp.zeros_like(high)
            pulled = jnp.zeros_like(high)
            for n in range(BLOCKS):
                part = total[n, :, mine] * jnp.exp2(top[n, :, mine] - high)
                amount += part
                pulled += part * mean[n, :, mine]
            if slot == 0:
                part = causal_stat[h, 1] * jnp.exp2(causal_stat[h, 0] - high)
                amount += part
                pulled += part * causal_stat[h, 2]
            stat_own[h, slot : slot + 1] = high + jnp.log2(amount)
            stat_own[h, RESPS + slot : RESPS + slot + 1] = pulled / amount

    stats = [
        [
            remote(stat_own.at[h], stat_in.at[h, s], stat_send.at[h, s], stat_recv.at[h, s], holder(s))
            for s in range(1, RESPS)
        ]
        for h in range(2)
    ]

    def all_stats(h):
        for copy in stats[h]:
            copy.wait_recv()
        for slot in range(RESPS):
            mine = slot_columns(h, slot)
            logs = [stat_own[h, slot : slot + 1]]
            means = [stat_own[h, RESPS + slot : RESPS + slot + 1]]
            for s in range(1, RESPS):
                there = slot ^ s
                logs.append(stat_in[h, s, there : there + 1])
                means.append(stat_in[h, s, RESPS + there : RESPS + there + 1])
            high = jnp.maximum(jnp.maximum(logs[0], logs[1]), jnp.maximum(logs[2], logs[3]))
            parts = [jnp.exp2(value - high) for value in logs]
            amount = parts[0] + parts[1] + parts[2] + parts[3]
            pulled = parts[0] * means[0] + parts[1] * means[1] + parts[2] * means[2] + parts[3] * means[3]
            log_total[:, mine] = high + jnp.log2(amount)
            delta[:, mine] = pulled / amount

    lax.fori_loop(0, BLOCKS - 1, near_step, 0)
    take_relay(0)
    for n in range(BLOCKS - 1):
        score(n, 0, 1)
    take_share(BLOCKS - 1)
    pass_on(1)
    turn_keys(BLOCKS - 1)
    score(BLOCKS - 1, 0, 0)
    score(BLOCKS - 1, 0, 1)
    local_stats(0)
    for copy in stats[0]:
        copy.start()
    score(BLOCKS - 1, 1, 0)
    take_relay(1)

    def far_step(i, carry):
        score(2 * i, 1, 1)
        score(2 * i + 1, 1, 1)
        return carry

    lax.fori_loop(0, BLOCKS // 2, far_step, 0)
    local_stats(1)
    for copy in stats[1]:
        copy.start()
    dk_sum[...] = jnp.zeros_like(dk_sum)
    dv_sum[...] = jnp.zeros_like(dv_sum)
    all_stats(0)

    def second_pass(weights, pulled, high, centre, mine):
        attend = weights.astype(F32) * jnp.exp2(high - log_total[:, mine])
        slope = attend * (pulled.astype(F32) + (centre - delta[:, mine]))
        return attend.astype(BF16), slope.astype(BF16)

    def causal_gradients():
        dk = jnp.zeros((self_rows, wide), F32)
        dv = jnp.zeros((self_rows, wide), F32)
        for h in range(2):
            attend, slope = second_pass(
                causal_p[h], causal_d[h], causal_stat[h, 0], causal_stat[h, 2], slot_columns(h, 0)
            )
            dk += jnp.dot(slope, q_all[h, 0, :half], preferred_element_type=F32)
            dv += jnp.dot(attend, g_all[h, 0, :half], preferred_element_type=F32)
            dq_self[h] = jnp.dot(rk[...].T, slope, preferred_element_type=F32)
        self_flat[:, :wide] = dk * scaling
        self_flat[:, wide:] = dv

    def give(u):
        return remote(
            dq_part.at[u % 2, :, pl.ds(half, half)], dq_in.at[u], dq_send.at[u], dq_recv.at[u], holder(1)
        )

    def give_far(h):
        return remote(dq_far.at[h], dq_far_in.at[h], dq_far_send.at[h], dq_far_recv.at[h], holder(2))

    def send_far(h):
        give(2 * h).wait_recv()
        dq_far[h] = (dq_part[0, :, :half] + dq_in[2 * h]).astype(BF16)
        give_far(h).start()

    def fill_flat(h):
        give(2 * h + 1).wait_recv()
        give_far(h).wait_recv()
        whole = dq_part[1, :, :half] + dq_self[h] + dq_in[2 * h + 1] + dq_far_in[h].astype(F32)
        dq_rows[...] = (whole * scaling).T
        for i in range(group):
            flat[h, :, i * wide : (i + 1) * wide] = dq_rows[
                pl.ds(i, self_rows // 2, stride=group), :
            ].astype(BF16)
        both = self_flat[...].reshape(HEADS, 2, 8, 2 * wide)[:, h].reshape(self_rows // 2, 2 * wide)
        flat[h, :, group * wide :] = both.astype(BF16)

    def hidden_piece(h, t, there):
        return q_scaled.at[pl.ds(pl.multiple_of(((h * steps + t) * HEADS + there) * 32, 32), 32), :]

    def group_columns(t, k):
        return pl.ds(pl.multiple_of((t + (k // 2) * steps) * CHUNK + (k % 2) * narrow, narrow), narrow)

    def hidden_copy(h, t, e):
        there = head_index(e)
        back = (e // 4) * 4 + (4 - e % 4) % 4
        return remote(
            hidden_piece(h, t, there),
            hid_in.at[back - 1, h, t],
            hid_send.at[h, t, e],
            hid_recv.at[h, t, back],
            (there, resp),
        )

    def project(h, start, stop):
        def step(t, carry):
            v = 2 * (h * steps + t)
            for i in range(2):
                for load in weight_loads(v + i):
                    load.wait()
            sides = []
            for i in range(2):
                turned = lax.dot_general(weight[(v + i) % RING], flat[h], NT, preferred_element_type=F32)
                for k in range(2):
                    part = turned[k * narrow : (k + 1) * narrow].T
                    sides.append(part.reshape(HEADS, 1, 8, narrow))
            here = pl.ds(pl.multiple_of((h * steps + t) * HEADS * 32, 32), HEADS * 32)
            q_scaled[here, :] = jnp.concatenate(sides, axis=1).reshape(HEADS * 32, narrow).astype(BF16)
            for e in range(1, HEADS):
                hidden_copy(h, t, e).start()

            @pl.when(v + RING < 4 * steps)
            def _():
                for i in range(2):
                    for load in weight_loads(v + RING + i):
                        load.start()

            return carry

        lax.fori_loop(start, stop, step, 0)

    def to_owner(n):
        back, here, device = BACK[n], pl.ds(n * SHARE, SHARE), along_x(n)
        return [
            remote(v_all.at[here, :], dv_in.at[back - 1], dv_send.at[n], dv_recv.at[back], device),
            remote(k_all.at[here, :], dk_in.at[back - 1], dk_send.at[n], dk_recv.at[back], device),
        ]

    owed = [copy for n in range(1, BLOCKS) for copy in to_owner(n)]

    def gradient_unit(u, carry):
        h, pair = u // 2, 1 - u % 2
        mine = pair_columns(h, pair)

        @pl.when(u > 1)
        def _():
            give(u - 2).wait_send()

        for n in range(BLOCKS):
            here = pl.ds(n * SHARE, SHARE)
            attend, slope = second_pass(prob[here, mine], grad[here, mine], top[n, :, mine], mean[n, :, mine], mine)
            prob[here, mine] = attend
            grad[here, mine] = slope
        dv_sum[...] += jnp.dot(prob[:, mine], g_all[h, pair], preferred_element_type=F32)
        dk_sum[...] += jnp.dot(grad[:, mine], q_all[h, pair], preferred_element_type=F32)
        dq_part[u % 2] = jnp.dot(k_turned[...], grad[:, mine], preferred_element_type=F32)
        give(u).start()

        @pl.when(u == 0)
        def _():
            all_stats(1)
            causal_gradients()
            send_far(0)

        @pl.when(u == 2)
        def _():
            fill_flat(0)
            send_far(1)

        return carry

    lax.fori_loop(0, 4, gradient_unit, 0)

    for copy in shares:
        copy.wait_send()
    v_all[...] = dv_sum[...].astype(BF16)
    k_all[...] = (dk_sum[...] * scaling).astype(BF16)
    for copy in owed:
        copy.start()
    project(0, 0, steps)
    fill_flat(1)
    project(1, 0, steps)

    for copy in owed:
        copy.wait_recv()
    dk = dk_sum[pl.ds(0, SHARE), :] * scaling
    dv = dv_sum[pl.ds(0, SHARE), :]
    for n in range(1, BLOCKS):
        dk = dk + dk_in[n - 1].astype(F32)
        dv = dv + dv_in[n - 1].astype(F32)
    dk_out[...] = dk.astype(BF16)
    dv_out[...] = dv.astype(BF16)

    def hidden_step(t, carry):
        sums = []
        for h in range(2):
            for e in range(1, HEADS):
                hidden_copy(h, t, e).wait()
            result = hidden_piece(h, t, head)[...].astype(F32)
            for e in range(1, HEADS):
                result = result + hid_in[e - 1, h, t].astype(F32)
            sums.append(result)
        for k in range(4):
            rows = [result[8 * k : 8 * k + 8] for result in sums]
            hidden_out[:, group_columns(t, k)] = jnp.concatenate(rows, axis=0).astype(BF16)
        return carry

    lax.fori_loop(0, steps, hidden_step, 0)

    sent = far[0] + far[1] + near[0] + near[1] + relays[0] + relays[1] + stats[0] + stats[1] + owed
    sent += [give(2), give(3)] + [give_far(0), give_far(1)]
    for copy in sent:
        copy.wait_send()


def finish_kernel(hidden_in, dk_in, dv_in, hidden_out, dk_out, dv_out):
    hidden_out[...] = hidden_in[...]
    dk_out[...] = dk_in[...]
    dv_out[...] = dv_in[...]


def per_device(
    queries, resp_keys, resp_values, out_grad, prefix_keys, prefix_values, w_query, w_key, w_value, resp_lengths
):
    self_rows, group, size = queries.shape[1:]
    rows = self_rows * group
    half = rows // 2
    width = w_query.shape[0]
    keys = BLOCKS * SHARE
    steps = width // CHUNK // 2
    vmem, dma = pltpu.VMEM, pltpu.SemaphoreType.DMA
    whole = pl.BlockSpec(memory_space=pltpu.VMEM)
    outputs = (
        jax.ShapeDtypeStruct((self_rows // HEADS, width), BF16),
        jax.ShapeDtypeStruct((SHARE, size), BF16),
        jax.ShapeDtypeStruct((SHARE, size), BF16),
    )
    results = pl.pallas_call(
        kernel,
        out_shape=outputs,
        in_specs=[pl.BlockSpec(memory_space=pltpu.SMEM)] + [pl.BlockSpec(memory_space=pl.ANY)] * 9,
        out_specs=(whole, whole, whole),
        scratch_shapes=[
            vmem((2, 2, rows, size), BF16),
            vmem((2, 2, rows, size), BF16),
            vmem((keys, size), BF16),
            vmem((keys, size), BF16),
            vmem((RESPS * rows, 2 * size), BF16),
            vmem((size, keys), BF16),
            vmem((keys, RESPS * rows), BF16),
            vmem((keys, RESPS * rows), BF16),
            vmem((BLOCKS, 1, RESPS * rows), F32),
            vmem((BLOCKS, 1, RESPS * rows), F32),
            vmem((BLOCKS, 1, RESPS * rows), F32),
            vmem((1, RESPS * rows), F32),
            vmem((1, RESPS * rows), F32),
            vmem((self_rows, size), BF16),
            vmem((self_rows, size), BF16),
            vmem((2, self_rows, half), BF16),
            vmem((2, self_rows, half), BF16),
            vmem((2, 3, 1, half), F32),
            vmem((2, 2 * RESPS, half), F32),
            vmem((2, RESPS, 2 * RESPS, half), F32),
            vmem((2, size, half), F32),
            vmem((2, size, rows), F32),
            vmem((4, size, half), F32),
            vmem((2, size, half), BF16),
            vmem((2, size, half), BF16),
            vmem((half, size), F32),
            vmem((self_rows, 2 * size), F32),
            vmem((2, self_rows // 2, (group + 2) * size), BF16),
            vmem((RING, CHUNK, (group + 2) * size), BF16),
            vmem((HEADS - 1, 2, steps, 2 * self_rows // HEADS, CHUNK // 2), BF16),
            vmem((keys, size), F32),
            vmem((keys, size), F32),
            vmem((BLOCKS - 1, SHARE, size), BF16),
            vmem((BLOCKS - 1, SHARE, size), BF16),
            dma((4 + 4 * HEADS,)),
            dma((RING, 3)),
            dma((2, 2)),
            dma((2, 2)),
            dma((2, 2)),
            dma((2, 2)),
            dma((2, 2)),
            dma((2, 2)),
            dma((BLOCKS,)),
            dma((BLOCKS,)),
            dma((BLOCKS,)),
            dma((BLOCKS,)),
            dma((2, RESPS)),
            dma((2, RESPS)),
            dma((4,)),
            dma((4,)),
            dma((2,)),
            dma((2,)),
            dma((BLOCKS,)),
            dma((BLOCKS,)),
            dma((BLOCKS,)),
            dma((BLOCKS,)),
            dma((2, steps, HEADS)),
            dma((2, steps, HEADS)),
        ],
        compiler_params=pltpu.CompilerParams(
            collective_id=0, has_side_effects=True, vmem_limit_bytes=65400 * 1024
        ),
    )(
        resp_lengths,
        queries.reshape(rows, size),
        out_grad.reshape(rows, size),
        resp_keys.reshape(self_rows, size),
        resp_values.reshape(self_rows, size),
        prefix_keys.reshape(SHARE, size),
        prefix_values.reshape(SHARE, size),
        w_query,
        w_key,
        w_value,
    )
    hidden, dk, dv = pl.pallas_call(
        finish_kernel, out_shape=outputs, in_specs=[whole] * 3, out_specs=(whole,) * 3
    )(*results)
    return hidden[None], dk[:, None], dv[:, None]


def solution(mesh):
    in_specs = (
        P("resp", None, "head", None),
        P("resp", None, "head", None),
        P("resp", None, "head", None),
        P("resp", None, "head", None),
        P("resp", "head", None),
        P("resp", "head", None),
        P(None, "head"),
        P(None, "head"),
        P(None, "head"),
        P(),
    )
    out_specs = (P("resp", "head", None), P("resp", "head", None), P("resp", "head", None))
    return jax.shard_map(
        per_device, mesh=mesh, in_specs=in_specs, out_specs=out_specs, check_vma=False
    )
```

```python
import math

import jax
import jax.numpy as jnp
from jax import lax
from jax.experimental import pallas as pl
from jax.experimental.pallas import tpu as pltpu
from jax.sharding import PartitionSpec as P

MESH = pl.DeviceIdType.MESH
NT = (((1,), (1,)), ((), ()))
F32, BF16 = jnp.float32, jnp.bfloat16
PLACES = (0, 1, 3, 2)
BACK = (0, 2, 1, 3)
BLOCKS = 4
RESPS = 4
HEADS = 8
SHARE = 512
CHUNK = 512
RING = 4


def kernel(
    lengths_hbm, q_hbm, g_hbm, rk_hbm, rv_hbm, k_hbm, v_hbm, wq_hbm, wk_hbm, wv_hbm,
    hidden_out, dk_out, dv_out,
    lengths, q_all, g_all, k_all, v_all, q_scaled, k_turned, prob, grad, top, total, mean,
    log_total, delta, rk, rv, causal_p, causal_d, causal_stat, stat_own, stat_in,
    dq_self, dq_part, dq_in, dq_far, dq_far_in, dq_rows, self_flat, flat, weight, hid_in,
    dk_sum, dv_sum, dk_in, dv_in,
    local_sem, weight_sem, q_send, q_recv, far_send, far_recv, relay_send, relay_recv, k_send, k_recv, v_send, v_recv,
    stat_send, stat_recv, dq_send, dq_recv, dq_far_send, dq_far_recv, dk_send, dk_recv, dv_send, dv_recv,
    hid_send, hid_recv,
):
    pair_rows, wide = q_all.shape[2:]
    half = pair_rows // 2
    self_rows = rk.shape[0]
    group = 2 * half // self_rows
    head = lax.axis_index("head")
    resp = lax.axis_index("resp")
    z_lo, y = head // 4, head % 4
    z_hi, x, core = resp // 8, (resp // 2) % 4, resp % 2
    scaling = wide ** -0.5
    log2e = math.log2(math.e)
    steps = hid_in.shape[2]
    narrow = CHUNK // 2

    def along_x(n):
        return (head, z_hi * 8 + ((x + PLACES[n]) % 4) * 2 + core)

    def holder(slot):
        z_there = (z_hi + slot // 2) % 2
        core_there = (core + slot % 2) % 2
        return (head, z_there * 8 + x * 2 + core_there)

    def head_index(e):
        return ((z_lo + e // 4) % 2) * 4 + (y + e % 4) % 4

    def first(h, held):
        return held.at[h, 0, pl.ds(0, half), :]

    loads = [
        pltpu.make_async_copy(source, target, local_sem.at[i])
        for i, (source, target) in enumerate(
            (
                (k_hbm, k_all.at[pl.ds(0, SHARE), :]),
                (v_hbm, v_all.at[pl.ds(0, SHARE), :]),
                (rk_hbm, rk),
                (rv_hbm, rv),
                (lengths_hbm, lengths),
            )
        )
    ]
    piece_rows = half // HEADS
    for h in range(2):
        for o in range(HEADS):
            for i, (source, held) in enumerate(((q_hbm, q_all), (g_hbm, g_all))):
                loads.append(
                    pltpu.make_async_copy(
                        source.at[pl.ds((2 * o + h) * piece_rows, piece_rows), :],
                        held.at[h, 0, pl.ds(o * piece_rows, piece_rows), :],
                        local_sem.at[5 + (h * HEADS + o) * 2 + i],
                    )
                )
    for load in loads:
        load.start()

    def weight_loads(v):
        slot, width = v % RING, group * wide
        piece = pl.ds(pl.multiple_of(((v // 2) % steps + (v % 2) * steps) * CHUNK, CHUNK), CHUNK)
        return [
            pltpu.make_async_copy(
                source.at[piece, :], weight.at[slot, :, pl.ds(start, size)], weight_sem.at[slot, j]
            )
            for j, (source, start, size) in enumerate(
                ((wq_hbm, 0, width), (wk_hbm, width, wide), (wv_hbm, width + wide, wide))
            )
        ]

    barrier = pltpu.get_barrier_semaphore()
    partners = [along_x(n) for n in range(1, BLOCKS)] + [holder(s) for s in range(1, RESPS)]
    partners += [(head_index(e), resp) for e in range(1, HEADS)]
    for partner in partners:
        pl.semaphore_signal(barrier, inc=1, device_id=partner, device_id_type=MESH)

    def row_of(h, count):
        return (count >> 6) * 16 + 8 * h + ((count & 63) >> 3)

    for load in loads:
        load.wait()
    for h in range(2):
        place = lax.broadcasted_iota(jnp.int32, (half, 1), 0)
        live = row_of(h, place) < lengths[resp]
        g_all[h, 0, :half] = jnp.where(live, g_all[h, 0, :half], jnp.zeros((half, wide), BF16))

    pl.semaphore_wait(barrier, len(partners))

    def remote(source, target, send, recv, device):
        return pltpu.make_async_remote_copy(
            src_ref=source, dst_ref=target, send_sem=send, recv_sem=recv, device_id=device, device_id_type=MESH
        )

    def block(n):
        return pl.ds(pl.multiple_of(n * SHARE, SHARE), SHARE)

    def rows_to(h, origin, target, send, recv, device):
        (pair, at), (pair_there, at_there) = origin, target
        return [
            remote(
                held.at[h, pair, pl.ds(at * half, half), :],
                held.at[h, pair_there, pl.ds(at_there * half, half), :],
                send.at[h, i],
                recv.at[h, i],
                device,
            )
            for i, held in enumerate((q_all, g_all))
        ]

    far = [rows_to(h, (0, 0), (1, 0), far_send, far_recv, holder(2)) for h in range(2)]
    near = [rows_to(h, (0, 0), (0, 1), q_send, q_recv, holder(1)) for h in range(2)]
    relays = [rows_to(h, (1, 0), (1, 1), relay_send, relay_recv, holder(1)) for h in range(2)]
    for copy in far[0] + near[0] + near[1]:
        copy.start()
    shares = []
    for n in range(1, BLOCKS):
        there, here = pl.ds(BACK[n] * SHARE, SHARE), pl.ds(0, SHARE)
        for held, send, recv in ((k_all, k_send, k_recv), (v_all, v_send, v_recv)):
            copy = remote(held.at[here, :], held.at[there, :], send.at[n], recv.at[BACK[n]], along_x(n))
            copy.start()
            shares.append(copy)
    for copy in far[1]:
        copy.start()
    for v in range(RING):
        for load in weight_loads(v):
            load.start()

    def scale_queries(h, pair, at):
        piece = pl.ds(at * half, half)
        exact = q_all[h, pair, piece, :].astype(F32) * (scaling * log2e)
        high = exact.astype(BF16)
        here = pl.ds((2 * h + pair) * pair_rows + at * half, half)
        q_scaled[here, :wide] = high
        q_scaled[here, wide:] = (exact - high.astype(F32)).astype(BF16)

    def first_pass(keys, values, scaled, pulls, allowed):
        twice = jnp.concatenate([keys, keys], axis=1)
        scores = lax.dot_general(twice, scaled, NT, preferred_element_type=F32)
        if allowed is not None:
            scores = jnp.where(allowed, scores, -1e30)
        pulled = lax.dot_general(values, pulls, NT, preferred_element_type=F32)
        high = jnp.max(scores, axis=0, keepdims=True)
        weights = jnp.exp2(scores - high)
        amount = jnp.sum(weights, axis=0, keepdims=True)
        centre = jnp.sum(weights * pulled, axis=0, keepdims=True) / amount
        return weights.astype(BF16), (pulled - centre).astype(BF16), high, amount, centre

    def pair_columns(h, pair):
        return pl.ds(pl.multiple_of((2 * h + pair) * pair_rows, pair_rows), pair_rows)

    def slot_columns(h, slot):
        return pl.ds((RESPS * h + slot) * half, half)

    def score(n, h, pair):
        here, mine = block(n), pair_columns(h, pair)
        prob[here, mine], grad[here, mine], high, amount, centre = first_pass(
            k_all[here, :], v_all[here, :], q_scaled[mine, :], g_all[h, pair], None
        )
        top[n, :, mine] = high
        total[n, :, mine] = amount
        mean[n, :, mine] = centre

    def take_share(n):
        here = block(n)
        for held, send, recv in ((k_all, k_send, k_recv), (v_all, v_send, v_recv)):
            remote(held.at[here, :], held.at[here, :], send.at[n], recv.at[n], holder(1)).wait_recv()

    def turn_keys(n):
        here = block(n)
        k_turned[:, here] = k_all[here, :].T

    def pass_on(h):
        for copy in far[h]:
            copy.wait_recv()
        for copy in relays[h]:
            copy.start()

    def take_relay(h):
        scale_queries(h, 1, 0)
        for copy in relays[h]:
            copy.wait_recv()
        scale_queries(h, 1, 1)

    for h in range(2):
        scale_queries(h, 0, 0)
        key_place = lax.broadcasted_iota(jnp.int32, (self_rows, half), 0)
        row_place = row_of(h, lax.broadcasted_iota(jnp.int32, (self_rows, half), 1))
        causal_p[h], causal_d[h], high, amount, centre = first_pass(
            rk[...], rv[...], q_scaled[pl.ds(2 * h * pair_rows, half), :], g_all[h, 0, :half], key_place <= row_place
        )
        causal_stat[h, 0], causal_stat[h, 1], causal_stat[h, 2] = high, amount, centre
    for copy in near[0] + near[1]:
        copy.wait_recv()
    scale_queries(0, 0, 1)
    scale_queries(1, 0, 1)

    def near_step(n, carry):
        @pl.when(n > 0)
        def _():
            take_share(n)

        @pl.when(n == 2)
        def _():
            pass_on(0)

        turn_keys(n)
        score(n, 0, 0)
        score(n, 1, 0)
        return carry

    def local_stats(h):
        for slot in range(RESPS):
            mine = slot_columns(h, slot)
            high = top[0, :, mine]
            for n in range(1, BLOCKS):
                high = jnp.maximum(high, top[n, :, mine])
            if slot == 0:
                high = jnp.maximum(high, causal_stat[h, 0])
            amount = jnp.zeros_like(high)
            pulled = jnp.zeros_like(high)
            for n in range(BLOCKS):
                part = total[n, :, mine] * jnp.exp2(top[n, :, mine] - high)
                amount += part
                pulled += part * mean[n, :, mine]
            if slot == 0:
                part = causal_stat[h, 1] * jnp.exp2(causal_stat[h, 0] - high)
                amount += part
                pulled += part * causal_stat[h, 2]
            stat_own[h, slot : slot + 1] = high + jnp.log2(amount)
            stat_own[h, RESPS + slot : RESPS + slot + 1] = pulled / amount

    stats = [
        [
            remote(stat_own.at[h], stat_in.at[h, s], stat_send.at[h, s], stat_recv.at[h, s], holder(s))
            for s in range(1, RESPS)
        ]
        for h in range(2)
    ]

    def all_stats(h):
        for copy in stats[h]:
            copy.wait_recv()
        for slot in range(RESPS):
            mine = slot_columns(h, slot)
            logs = [stat_own[h, slot : slot + 1]]
            means = [stat_own[h, RESPS + slot : RESPS + slot + 1]]
            for s in range(1, RESPS):
                there = slot ^ s
                logs.append(stat_in[h, s, there : there + 1])
                means.append(stat_in[h, s, RESPS + there : RESPS + there + 1])
            high = jnp.maximum(jnp.maximum(logs[0], logs[1]), jnp.maximum(logs[2], logs[3]))
            parts = [jnp.exp2(value - high) for value in logs]
            amount = parts[0] + parts[1] + parts[2] + parts[3]
            pulled = parts[0] * means[0] + parts[1] * means[1] + parts[2] * means[2] + parts[3] * means[3]
            log_total[:, mine] = high + jnp.log2(amount)
            delta[:, mine] = pulled / amount

    lax.fori_loop(0, BLOCKS - 1, near_step, 0)
    take_relay(0)
    for n in range(BLOCKS - 1):
        score(n, 0, 1)
    take_share(BLOCKS - 1)
    pass_on(1)
    turn_keys(BLOCKS - 1)
    score(BLOCKS - 1, 0, 0)
    score(BLOCKS - 1, 0, 1)
    local_stats(0)
    for copy in stats[0]:
        copy.start()
    score(BLOCKS - 1, 1, 0)
    take_relay(1)

    def far_step(i, carry):
        score(2 * i, 1, 1)
        score(2 * i + 1, 1, 1)
        return carry

    lax.fori_loop(0, BLOCKS // 2, far_step, 0)
    local_stats(1)
    for copy in stats[1]:
        copy.start()
    dk_sum[...] = jnp.zeros_like(dk_sum)
    dv_sum[...] = jnp.zeros_like(dv_sum)
    all_stats(0)

    def second_pass(weights, pulled, high, centre, mine):
        attend = weights.astype(F32) * jnp.exp2(high - log_total[:, mine])
        slope = attend * (pulled.astype(F32) + (centre - delta[:, mine]))
        return attend.astype(BF16), slope.astype(BF16)

    def causal_gradients():
        dk = jnp.zeros((self_rows, wide), F32)
        dv = jnp.zeros((self_rows, wide), F32)
        for h in range(2):
            attend, slope = second_pass(
                causal_p[h], causal_d[h], causal_stat[h, 0], causal_stat[h, 2], slot_columns(h, 0)
            )
            dk += jnp.dot(slope, q_all[h, 0, :half], preferred_element_type=F32)
            dv += jnp.dot(attend, g_all[h, 0, :half], preferred_element_type=F32)
            turned = jnp.dot(rk[...].T, slope, preferred_element_type=F32)
            dq_self[h] = turned if h else dq_self[h] + turned
        self_flat[:, :wide] = dk * scaling
        self_flat[:, wide:] = dv

    def give(u):
        return remote(
            dq_part.at[u % 2, :, pl.ds(half, half)], dq_in.at[u], dq_send.at[u], dq_recv.at[u], holder(1)
        )

    def give_far(h):
        return remote(dq_far.at[h], dq_far_in.at[h], dq_far_send.at[h], dq_far_recv.at[h], holder(2))

    def send_far(h):
        give(2 * h).wait_recv()
        dq_far[h] = (dq_part[0, :, :half] + dq_in[2 * h]).astype(BF16)
        give_far(h).start()

    def fill_flat(h):
        give(2 * h + 1).wait_recv()
        give_far(h).wait_recv()
        whole = dq_self[h] + dq_in[2 * h + 1] + dq_far_in[h].astype(F32)
        if h:
            whole = whole + dq_part[1, :, :half]
        dq_rows[...] = (whole * scaling).T
        for i in range(group):
            flat[h, :, i * wide : (i + 1) * wide] = dq_rows[
                pl.ds(i, self_rows // 2, stride=group), :
            ].astype(BF16)
        both = self_flat[...].reshape(HEADS, 2, 8, 2 * wide)[:, h].reshape(self_rows // 2, 2 * wide)
        flat[h, :, group * wide :] = both.astype(BF16)

    def hidden_piece(h, t, there):
        return q_scaled.at[pl.ds(pl.multiple_of(((h * steps + t) * HEADS + there) * 32, 32), 32), :]

    def group_columns(t, k):
        return pl.ds(pl.multiple_of((t + (k // 2) * steps) * CHUNK + (k % 2) * narrow, narrow), narrow)

    def hidden_copy(h, t, e):
        there = head_index(e)
        back = (e // 4) * 4 + (4 - e % 4) % 4
        return remote(
            hidden_piece(h, t, there),
            hid_in.at[back - 1, h, t],
            hid_send.at[h, t, e],
            hid_recv.at[h, t, back],
            (there, resp),
        )

    def project(h, start, stop):
        def step(t, carry):
            v = 2 * (h * steps + t)
            for i in range(2):
                for load in weight_loads(v + i):
                    load.wait()
            sides = []
            for i in range(2):
                turned = lax.dot_general(weight[(v + i) % RING], flat[h], NT, preferred_element_type=F32)
                for k in range(2):
                    part = turned[k * narrow : (k + 1) * narrow].T
                    sides.append(part.reshape(HEADS, 1, 8, narrow))
            here = pl.ds(pl.multiple_of((h * steps + t) * HEADS * 32, 32), HEADS * 32)
            q_scaled[here, :] = jnp.concatenate(sides, axis=1).reshape(HEADS * 32, narrow).astype(BF16)
            for e in range(1, HEADS):
                hidden_copy(h, t, e).start()

            @pl.when(v + RING < 4 * steps)
            def _():
                for i in range(2):
                    for load in weight_loads(v + RING + i):
                        load.start()

            return carry

        lax.fori_loop(start, stop, step, 0)

    def to_owner(n):
        back, here, device = BACK[n], pl.ds(n * SHARE, SHARE), along_x(n)
        return [
            remote(v_all.at[here, :], dv_in.at[back - 1], dv_send.at[n], dv_recv.at[back], device),
            remote(k_all.at[here, :], dk_in.at[back - 1], dk_send.at[n], dk_recv.at[back], device),
        ]

    owed = [copy for n in range(1, BLOCKS) for copy in to_owner(n)]

    def gradient_unit(u, carry):
        h, pair = u // 2, 1 - u % 2
        mine = pair_columns(h, pair)

        @pl.when(u > 1)
        def _():
            give(u - 2).wait_send()

        slopes = []
        for n in range(BLOCKS):
            here = pl.ds(n * SHARE, SHARE)
            attend, slope = second_pass(prob[here, mine], grad[here, mine], top[n, :, mine], mean[n, :, mine], mine)
            dv_sum[here, :] += jnp.dot(attend, g_all[h, pair], preferred_element_type=F32)
            dk_sum[here, :] += jnp.dot(slope, q_all[h, pair], preferred_element_type=F32)
            slopes.append(slope)
        slopes = jnp.concatenate(slopes, axis=0)
        dq_part[u % 2] = jnp.dot(k_turned[...], slopes, preferred_element_type=F32)
        give(u).start()

        @pl.when(u == 0)
        def _():
            all_stats(1)

        @pl.when(u == 1)
        def _():
            dq_self[0] = dq_part[1, :, :half]
            send_far(0)

        @pl.when(u == 2)
        def _():
            causal_gradients()
            send_far(1)

        return carry

    lax.fori_loop(0, 4, gradient_unit, 0)

    for copy in shares:
        copy.wait_send()
    v_all[...] = dv_sum[...].astype(BF16)
    k_all[...] = (dk_sum[...] * scaling).astype(BF16)
    for copy in owed:
        copy.start()
    fill_flat(0)
    project(0, 0, steps)
    fill_flat(1)
    project(1, 0, steps)

    for copy in owed:
        copy.wait_recv()
    dk = dk_sum[pl.ds(0, SHARE), :] * scaling
    dv = dv_sum[pl.ds(0, SHARE), :]
    for n in range(1, BLOCKS):
        dk = dk + dk_in[n - 1].astype(F32)
        dv = dv + dv_in[n - 1].astype(F32)
    dk_out[...] = dk.astype(BF16)
    dv_out[...] = dv.astype(BF16)

    def hidden_step(t, carry):
        sums = []
        for h in range(2):
            for e in range(1, HEADS):
                hidden_copy(h, t, e).wait()
            result = hidden_piece(h, t, head)[...].astype(F32)
            for e in range(1, HEADS):
                result = result + hid_in[e - 1, h, t].astype(F32)
            sums.append(result)
        for k in range(4):
            rows = [result[8 * k : 8 * k + 8] for result in sums]
            hidden_out[:, group_columns(t, k)] = jnp.concatenate(rows, axis=0).astype(BF16)
        return carry

    lax.fori_loop(0, steps, hidden_step, 0)

    sent = far[0] + far[1] + near[0] + near[1] + relays[0] + relays[1] + stats[0] + stats[1] + owed
    sent += [give(2), give(3)] + [give_far(0), give_far(1)]
    for copy in sent:
        copy.wait_send()


def finish_kernel(hidden_in, dk_in, dv_in, hidden_out, dk_out, dv_out):
    hidden_out[...] = hidden_in[...]
    dk_out[...] = dk_in[...]
    dv_out[...] = dv_in[...]


def per_device(
    queries, resp_keys, resp_values, out_grad, prefix_keys, prefix_values, w_query, w_key, w_value, resp_lengths
):
    self_rows, group, size = queries.shape[1:]
    rows = self_rows * group
    half = rows // 2
    width = w_query.shape[0]
    keys = BLOCKS * SHARE
    steps = width // CHUNK // 2
    vmem, dma = pltpu.VMEM, pltpu.SemaphoreType.DMA
    whole = pl.BlockSpec(memory_space=pltpu.VMEM)
    outputs = (
        jax.ShapeDtypeStruct((self_rows // HEADS, width), BF16),
        jax.ShapeDtypeStruct((SHARE, size), BF16),
        jax.ShapeDtypeStruct((SHARE, size), BF16),
    )
    results = pl.pallas_call(
        kernel,
        out_shape=outputs,
        in_specs=[pl.BlockSpec(memory_space=pl.ANY)] * 10,
        out_specs=(whole, whole, whole),
        scratch_shapes=[
            pltpu.SMEM(resp_lengths.shape, jnp.int32),
            vmem((2, 2, rows, size), BF16),
            vmem((2, 2, rows, size), BF16),
            vmem((keys, size), BF16),
            vmem((keys, size), BF16),
            vmem((RESPS * rows, 2 * size), BF16),
            vmem((size, keys), BF16),
            vmem((keys, RESPS * rows), BF16),
            vmem((keys, RESPS * rows), BF16),
            vmem((BLOCKS, 1, RESPS * rows), F32),
            vmem((BLOCKS, 1, RESPS * rows), F32),
            vmem((BLOCKS, 1, RESPS * rows), F32),
            vmem((1, RESPS * rows), F32),
            vmem((1, RESPS * rows), F32),
            vmem((self_rows, size), BF16),
            vmem((self_rows, size), BF16),
            vmem((2, self_rows, half), BF16),
            vmem((2, self_rows, half), BF16),
            vmem((2, 3, 1, half), F32),
            vmem((2, 2 * RESPS, half), F32),
            vmem((2, RESPS, 2 * RESPS, half), F32),
            vmem((2, size, half), F32),
            vmem((2, size, rows), F32),
            vmem((4, size, half), F32),
            vmem((2, size, half), BF16),
            vmem((2, size, half), BF16),
            vmem((half, size), F32),
            vmem((self_rows, 2 * size), F32),
            vmem((2, self_rows // 2, (group + 2) * size), BF16),
            vmem((RING, CHUNK, (group + 2) * size), BF16),
            vmem((HEADS - 1, 2, steps, 2 * self_rows // HEADS, CHUNK // 2), BF16),
            vmem((keys, size), F32),
            vmem((keys, size), F32),
            vmem((BLOCKS - 1, SHARE, size), BF16),
            vmem((BLOCKS - 1, SHARE, size), BF16),
            dma((5 + 4 * HEADS,)),
            dma((RING, 3)),
            dma((2, 2)),
            dma((2, 2)),
            dma((2, 2)),
            dma((2, 2)),
            dma((2, 2)),
            dma((2, 2)),
            dma((BLOCKS,)),
            dma((BLOCKS,)),
            dma((BLOCKS,)),
            dma((BLOCKS,)),
            dma((2, RESPS)),
            dma((2, RESPS)),
            dma((4,)),
            dma((4,)),
            dma((2,)),
            dma((2,)),
            dma((BLOCKS,)),
            dma((BLOCKS,)),
            dma((BLOCKS,)),
            dma((BLOCKS,)),
            dma((2, steps, HEADS)),
            dma((2, steps, HEADS)),
        ],
        compiler_params=pltpu.CompilerParams(
            collective_id=0, has_side_effects=True, vmem_limit_bytes=65400 * 1024
        ),
    )(
        resp_lengths,
        queries.reshape(rows, size),
        out_grad.reshape(rows, size),
        resp_keys.reshape(self_rows, size),
        resp_values.reshape(self_rows, size),
        prefix_keys.reshape(SHARE, size),
        prefix_values.reshape(SHARE, size),
        w_query,
        w_key,
        w_value,
    )
    hidden, dk, dv = pl.pallas_call(
        finish_kernel, out_shape=outputs, in_specs=[whole] * 3, out_specs=(whole,) * 3
    )(*results)
    return hidden[None], dk[:, None], dv[:, None]


def solution(mesh):
    in_specs = (
        P("resp", None, "head", None),
        P("resp", None, "head", None),
        P("resp", None, "head", None),
        P("resp", None, "head", None),
        P("resp", "head", None),
        P("resp", "head", None),
        P(None, "head"),
        P(None, "head"),
        P(None, "head"),
        P(),
    )
    out_specs = (P("resp", "head", None), P("resp", "head", None), P("resp", "head", None))
    return jax.shard_map(
        per_device, mesh=mesh, in_specs=in_specs, out_specs=out_specs, check_vma=False
    )
```

```python
import math

import jax
import jax.numpy as jnp
from jax import lax
from jax.experimental import pallas as pl
from jax.experimental.pallas import tpu as pltpu
from jax.sharding import PartitionSpec as P

MESH = pl.DeviceIdType.MESH
NT = (((1,), (1,)), ((), ()))
F32, BF16 = jnp.float32, jnp.bfloat16
PLACES = (0, 1, 3, 2)
BACK = (0, 2, 1, 3)
BLOCKS = 4
RESPS = 4
HEADS = 8
SHARE = 512
CHUNK = 512
RING = 4


def kernel(
    lengths_hbm, q_hbm, g_hbm, rk_hbm, rv_hbm, k_hbm, v_hbm, wq_hbm, wk_hbm, wv_hbm,
    hidden_out, dk_out, dv_out,
    lengths, q_all, g_all, k_all, v_all, q_scaled, k_turned, prob, grad, top, total, mean,
    log_total, delta, rk, rv, causal_p, causal_d, causal_stat, stat_own, stat_in,
    dq_self, dq_part, dq_in, dq_far, dq_far_in, dq_rows, self_flat, flat, weight, hid_in,
    dk_sum, dv_sum, dk_in, dv_in,
    local_sem, weight_sem, q_send, q_recv, far_send, far_recv, relay_send, relay_recv, k_send, k_recv, v_send, v_recv,
    stat_send, stat_recv, dq_send, dq_recv, dq_far_send, dq_far_recv, dk_send, dk_recv, dv_send, dv_recv,
    hid_send, hid_recv,
):
    pair_rows, wide = q_all.shape[2:]
    half = pair_rows // 2
    self_rows = rk.shape[0]
    group = 2 * half // self_rows
    head = lax.axis_index("head")
    resp = lax.axis_index("resp")
    z_lo, y = head // 4, head % 4
    z_hi, x, core = resp // 8, (resp // 2) % 4, resp % 2
    scaling = wide ** -0.5
    log2e = math.log2(math.e)
    steps = hid_in.shape[2]
    narrow = CHUNK // 2

    def along_x(n):
        return (head, z_hi * 8 + ((x + PLACES[n]) % 4) * 2 + core)

    def holder(slot):
        z_there = (z_hi + slot // 2) % 2
        core_there = (core + slot % 2) % 2
        return (head, z_there * 8 + x * 2 + core_there)

    def head_index(e):
        return ((z_lo + e // 4) % 2) * 4 + (y + e % 4) % 4

    def first(h, held):
        return held.at[h, 0, pl.ds(0, half), :]

    loads = [
        pltpu.make_async_copy(source, target, local_sem.at[i])
        for i, (source, target) in enumerate(
            (
                (k_hbm, k_all.at[pl.ds(0, SHARE), :]),
                (v_hbm, v_all.at[pl.ds(0, SHARE), :]),
                (rk_hbm, rk),
                (rv_hbm, rv),
                (lengths_hbm, lengths),
            )
        )
    ]
    piece_rows = half // HEADS
    for h in range(2):
        for o in range(HEADS):
            for i, (source, held) in enumerate(((q_hbm, q_all), (g_hbm, g_all))):
                loads.append(
                    pltpu.make_async_copy(
                        source.at[pl.ds((2 * o + h) * piece_rows, piece_rows), :],
                        held.at[h, 0, pl.ds(o * piece_rows, piece_rows), :],
                        local_sem.at[5 + (h * HEADS + o) * 2 + i],
                    )
                )
    for load in loads:
        load.start()

    def weight_loads(v):
        slot, width = v % RING, group * wide
        piece = pl.ds(pl.multiple_of(((v // 2) % steps + (v % 2) * steps) * CHUNK, CHUNK), CHUNK)
        return [
            pltpu.make_async_copy(
                source.at[piece, :], weight.at[slot, :, pl.ds(start, size)], weight_sem.at[slot, j]
            )
            for j, (source, start, size) in enumerate(
                ((wq_hbm, 0, width), (wk_hbm, width, wide), (wv_hbm, width + wide, wide))
            )
        ]

    barrier = pltpu.get_barrier_semaphore()
    partners = [along_x(n) for n in range(1, BLOCKS)] + [holder(s) for s in range(1, RESPS)]
    partners += [(head_index(e), resp) for e in range(1, HEADS)]
    for partner in partners:
        pl.semaphore_signal(barrier, inc=1, device_id=partner, device_id_type=MESH)

    def row_of(h, count):
        return (count >> 6) * 16 + 8 * h + ((count & 63) >> 3)

    for load in loads:
        load.wait()
    for h in range(2):
        place = lax.broadcasted_iota(jnp.int32, (half, 1), 0)
        live = row_of(h, place) < lengths[resp]
        g_all[h, 0, :half] = jnp.where(live, g_all[h, 0, :half], jnp.zeros((half, wide), BF16))

    pl.semaphore_wait(barrier, len(partners))

    def remote(source, target, send, recv, device):
        return pltpu.make_async_remote_copy(
            src_ref=source, dst_ref=target, send_sem=send, recv_sem=recv, device_id=device, device_id_type=MESH
        )

    def block(n):
        return pl.ds(pl.multiple_of(n * SHARE, SHARE), SHARE)

    def rows_to(h, origin, target, send, recv, device):
        (pair, at), (pair_there, at_there) = origin, target
        return [
            remote(
                held.at[h, pair, pl.ds(at * half, half), :],
                held.at[h, pair_there, pl.ds(at_there * half, half), :],
                send.at[h, i],
                recv.at[h, i],
                device,
            )
            for i, held in enumerate((q_all, g_all))
        ]

    far = [rows_to(h, (0, 0), (1, 0), far_send, far_recv, holder(2)) for h in range(2)]
    near = [rows_to(h, (0, 0), (0, 1), q_send, q_recv, holder(1)) for h in range(2)]
    relays = [rows_to(h, (1, 0), (1, 1), relay_send, relay_recv, holder(1)) for h in range(2)]
    for copy in far[0] + near[0] + near[1]:
        copy.start()
    shares = []
    for n in range(1, BLOCKS):
        there, here = pl.ds(BACK[n] * SHARE, SHARE), pl.ds(0, SHARE)
        for held, send, recv in ((k_all, k_send, k_recv), (v_all, v_send, v_recv)):
            copy = remote(held.at[here, :], held.at[there, :], send.at[n], recv.at[BACK[n]], along_x(n))
            copy.start()
            shares.append(copy)
    for copy in far[1]:
        copy.start()
    for v in range(RING):
        for load in weight_loads(v):
            load.start()

    def scale_queries(h, pair, at):
        piece = pl.ds(at * half, half)
        exact = q_all[h, pair, piece, :].astype(F32) * (scaling * log2e)
        high = exact.astype(BF16)
        here = pl.ds((2 * h + pair) * pair_rows + at * half, half)
        q_scaled[here, :wide] = high
        q_scaled[here, wide:] = (exact - high.astype(F32)).astype(BF16)

    def first_pass(keys, values, scaled, pulls, allowed):
        twice = jnp.concatenate([keys, keys], axis=1)
        scores = lax.dot_general(twice, scaled, NT, preferred_element_type=F32)
        if allowed is not None:
            scores = jnp.where(allowed, scores, -1e30)
        pulled = lax.dot_general(values, pulls, NT, preferred_element_type=F32)
        high = jnp.max(scores, axis=0, keepdims=True)
        weights = jnp.exp2(scores - high)
        amount = jnp.sum(weights, axis=0, keepdims=True)
        centre = jnp.sum(weights * pulled, axis=0, keepdims=True) / amount
        return weights.astype(BF16), (pulled - centre).astype(BF16), high, amount, centre

    def pair_columns(h, pair):
        return pl.ds(pl.multiple_of((2 * h + pair) * pair_rows, pair_rows), pair_rows)

    def slot_columns(h, slot):
        return pl.ds((RESPS * h + slot) * half, half)

    def score(n, h, pair):
        here, mine = block(n), pair_columns(h, pair)
        prob[here, mine], grad[here, mine], high, amount, centre = first_pass(
            k_all[here, :], v_all[here, :], q_scaled[mine, :], g_all[h, pair], None
        )
        top[n, :, mine] = high
        total[n, :, mine] = amount
        mean[n, :, mine] = centre

    def take_share(n):
        here = block(n)
        for held, send, recv in ((k_all, k_send, k_recv), (v_all, v_send, v_recv)):
            remote(held.at[here, :], held.at[here, :], send.at[n], recv.at[n], holder(1)).wait_recv()

    def turn_keys(n):
        here = block(n)
        k_turned[:, here] = k_all[here, :].T

    def pass_on(h):
        for copy in far[h]:
            copy.wait_recv()
        for copy in relays[h]:
            copy.start()

    def take_relay(h):
        scale_queries(h, 1, 0)
        for copy in relays[h]:
            copy.wait_recv()
        scale_queries(h, 1, 1)

    for h in range(2):
        scale_queries(h, 0, 0)
        key_place = lax.broadcasted_iota(jnp.int32, (self_rows, half), 0)
        row_place = row_of(h, lax.broadcasted_iota(jnp.int32, (self_rows, half), 1))
        causal_p[h], causal_d[h], high, amount, centre = first_pass(
            rk[...], rv[...], q_scaled[pl.ds(2 * h * pair_rows, half), :], g_all[h, 0, :half], key_place <= row_place
        )
        causal_stat[h, 0], causal_stat[h, 1], causal_stat[h, 2] = high, amount, centre
    for copy in near[0] + near[1]:
        copy.wait_recv()
    scale_queries(0, 0, 1)
    scale_queries(1, 0, 1)

    def near_step(n, carry):
        @pl.when(n > 0)
        def _():
            take_share(n)

        @pl.when(n == 2)
        def _():
            pass_on(0)

        turn_keys(n)
        score(n, 0, 0)
        score(n, 1, 0)
        return carry

    def local_stats(h):
        for slot in range(RESPS):
            mine = slot_columns(h, slot)
            high = top[0, :, mine]
            for n in range(1, BLOCKS):
                high = jnp.maximum(high, top[n, :, mine])
            if slot == 0:
                high = jnp.maximum(high, causal_stat[h, 0])
            amount = jnp.zeros_like(high)
            pulled = jnp.zeros_like(high)
            for n in range(BLOCKS):
                part = total[n, :, mine] * jnp.exp2(top[n, :, mine] - high)
                amount += part
                pulled += part * mean[n, :, mine]
            if slot == 0:
                part = causal_stat[h, 1] * jnp.exp2(causal_stat[h, 0] - high)
                amount += part
                pulled += part * causal_stat[h, 2]
            stat_own[h, slot : slot + 1] = high + jnp.log2(amount)
            stat_own[h, RESPS + slot : RESPS + slot + 1] = pulled / amount

    stats = [
        [
            remote(stat_own.at[h], stat_in.at[h, s], stat_send.at[h, s], stat_recv.at[h, s], holder(s))
            for s in range(1, RESPS)
        ]
        for h in range(2)
    ]

    def all_stats(h):
        for copy in stats[h]:
            copy.wait_recv()
        for slot in range(RESPS):
            mine = slot_columns(h, slot)
            logs = [stat_own[h, slot : slot + 1]]
            means = [stat_own[h, RESPS + slot : RESPS + slot + 1]]
            for s in range(1, RESPS):
                there = slot ^ s
                logs.append(stat_in[h, s, there : there + 1])
                means.append(stat_in[h, s, RESPS + there : RESPS + there + 1])
            high = jnp.maximum(jnp.maximum(logs[0], logs[1]), jnp.maximum(logs[2], logs[3]))
            parts = [jnp.exp2(value - high) for value in logs]
            amount = parts[0] + parts[1] + parts[2] + parts[3]
            pulled = parts[0] * means[0] + parts[1] * means[1] + parts[2] * means[2] + parts[3] * means[3]
            log_total[:, mine] = high + jnp.log2(amount)
            delta[:, mine] = pulled / amount

    lax.fori_loop(0, BLOCKS - 1, near_step, 0)
    take_relay(0)
    for n in range(BLOCKS - 1):
        score(n, 0, 1)
    take_share(BLOCKS - 1)
    pass_on(1)
    turn_keys(BLOCKS - 1)
    score(BLOCKS - 1, 0, 0)
    score(BLOCKS - 1, 0, 1)
    local_stats(0)
    for copy in stats[0]:
        copy.start()
    score(BLOCKS - 1, 1, 0)
    take_relay(1)

    def far_step(i, carry):
        score(2 * i, 1, 1)
        score(2 * i + 1, 1, 1)
        return carry

    lax.fori_loop(0, BLOCKS // 2, far_step, 0)
    local_stats(1)
    for copy in stats[1]:
        copy.start()
    dk_sum[...] = jnp.zeros_like(dk_sum)
    dv_sum[...] = jnp.zeros_like(dv_sum)
    all_stats(0)

    def second_pass(weights, pulled, high, centre, mine):
        attend = weights.astype(F32) * jnp.exp2(high - log_total[:, mine])
        slope = attend * (pulled.astype(F32) + (centre - delta[:, mine]))
        return attend.astype(BF16), slope.astype(BF16)

    def causal_gradients():
        dk = jnp.zeros((self_rows, wide), F32)
        dv = jnp.zeros((self_rows, wide), F32)
        for h in range(2):
            attend, slope = second_pass(
                causal_p[h], causal_d[h], causal_stat[h, 0], causal_stat[h, 2], slot_columns(h, 0)
            )
            dk += jnp.dot(slope, q_all[h, 0, :half], preferred_element_type=F32)
            dv += jnp.dot(attend, g_all[h, 0, :half], preferred_element_type=F32)
            turned = jnp.dot(rk[...].T, slope, preferred_element_type=F32)
            dq_self[h] = turned if h else dq_self[h] + turned
        self_flat[:, :wide] = dk * scaling
        self_flat[:, wide:] = dv

    def give(u):
        return remote(
            dq_part.at[u % 2, :, pl.ds(half, half)], dq_in.at[u], dq_send.at[u], dq_recv.at[u], holder(1)
        )

    def give_far(h):
        return remote(dq_far.at[h], dq_far_in.at[h], dq_far_send.at[h], dq_far_recv.at[h], holder(2))

    def send_far(h):
        give(2 * h).wait_recv()
        dq_far[h] = (dq_part[0, :, :half] + dq_in[2 * h]).astype(BF16)
        give_far(h).start()

    def fill_flat(h):
        give(2 * h + 1).wait_recv()
        give_far(h).wait_recv()
        whole = dq_self[h] + dq_in[2 * h + 1] + dq_far_in[h].astype(F32)
        if h:
            whole = whole + dq_part[1, :, :half]
        dq_rows[...] = (whole * scaling).T
        for i in range(group):
            flat[h, :, i * wide : (i + 1) * wide] = dq_rows[
                pl.ds(i, self_rows // 2, stride=group), :
            ].astype(BF16)
        both = self_flat[...].reshape(HEADS, 2, 8, 2 * wide)[:, h].reshape(self_rows // 2, 2 * wide)
        flat[h, :, group * wide :] = both.astype(BF16)

    def hidden_piece(h, t, there):
        return q_scaled.at[pl.ds(pl.multiple_of(((h * steps + t) * HEADS + there) * 32, 32), 32), :]

    def group_columns(t, k):
        return pl.ds(pl.multiple_of((t + (k // 2) * steps) * CHUNK + (k % 2) * narrow, narrow), narrow)

    def hidden_copy(h, t, e):
        there = head_index(e)
        back = (e // 4) * 4 + (4 - e % 4) % 4
        return remote(
            hidden_piece(h, t, there),
            hid_in.at[back - 1, h, t],
            hid_send.at[h, t, e],
            hid_recv.at[h, t, back],
            (there, resp),
        )

    def project(h, start, stop):
        def step(t, carry):
            v = 2 * (h * steps + t)
            for i in range(2):
                for load in weight_loads(v + i):
                    load.wait()
            sides = []
            for i in range(2):
                turned = lax.dot_general(weight[(v + i) % RING], flat[h], NT, preferred_element_type=F32)
                for k in range(2):
                    part = turned[k * narrow : (k + 1) * narrow].T
                    sides.append(part.reshape(HEADS, 1, 8, narrow))
            here = pl.ds(pl.multiple_of((h * steps + t) * HEADS * 32, 32), HEADS * 32)
            q_scaled[here, :] = jnp.concatenate(sides, axis=1).reshape(HEADS * 32, narrow).astype(BF16)
            @pl.when(v + RING < 4 * steps)
            def _():
                for i in range(2):
                    for load in weight_loads(v + RING + i):
                        load.start()

            for e in range(1, HEADS):
                hidden_copy(h, t, e).start()

            return carry

        lax.fori_loop(start, stop, step, 0)

    def to_owner(n):
        back, here, device = BACK[n], pl.ds(n * SHARE, SHARE), along_x(n)
        return [
            remote(v_all.at[here, :], dv_in.at[back - 1], dv_send.at[n], dv_recv.at[back], device),
            remote(k_all.at[here, :], dk_in.at[back - 1], dk_send.at[n], dk_recv.at[back], device),
        ]

    owed = [copy for n in range(1, BLOCKS) for copy in to_owner(n)]

    def gradient_unit(u, carry):
        h, pair = u // 2, 1 - u % 2
        mine = pair_columns(h, pair)

        @pl.when(u > 1)
        def _():
            give(u - 2).wait_send()

        slopes = []
        for n in range(BLOCKS):
            here = pl.ds(n * SHARE, SHARE)
            attend, slope = second_pass(prob[here, mine], grad[here, mine], top[n, :, mine], mean[n, :, mine], mine)
            dv_sum[here, :] += jnp.dot(attend, g_all[h, pair], preferred_element_type=F32)
            dk_sum[here, :] += jnp.dot(slope, q_all[h, pair], preferred_element_type=F32)
            slopes.append(slope)
        slopes = jnp.concatenate(slopes, axis=0)
        dq_part[u % 2] = jnp.dot(k_turned[...], slopes, preferred_element_type=F32)
        give(u).start()

        @pl.when(u == 0)
        def _():
            all_stats(1)

        @pl.when(u == 1)
        def _():
            dq_self[0] = dq_part[1, :, :half]
            send_far(0)

        @pl.when(u == 2)
        def _():
            causal_gradients()
            send_far(1)

        return carry

    lax.fori_loop(0, 4, gradient_unit, 0)

    for copy in shares:
        copy.wait_send()
    v_all[...] = dv_sum[...].astype(BF16)
    k_all[...] = (dk_sum[...] * scaling).astype(BF16)
    for copy in owed:
        copy.start()
    fill_flat(0)
    project(0, 0, steps)
    fill_flat(1)
    project(1, 0, steps)

    for copy in owed:
        copy.wait_recv()
    dk = dk_sum[pl.ds(0, SHARE), :] * scaling
    dv = dv_sum[pl.ds(0, SHARE), :]
    for n in range(1, BLOCKS):
        dk = dk + dk_in[n - 1].astype(F32)
        dv = dv + dv_in[n - 1].astype(F32)
    dk_out[...] = dk.astype(BF16)
    dv_out[...] = dv.astype(BF16)

    def hidden_step(t, carry):
        sums = []
        for h in range(2):
            for e in range(1, HEADS):
                hidden_copy(h, t, e).wait()
            result = hidden_piece(h, t, head)[...].astype(F32)
            for e in range(1, HEADS):
                result = result + hid_in[e - 1, h, t].astype(F32)
            sums.append(result)
        for k in range(4):
            rows = [result[8 * k : 8 * k + 8] for result in sums]
            hidden_out[:, group_columns(t, k)] = jnp.concatenate(rows, axis=0).astype(BF16)
        return carry

    lax.fori_loop(0, steps, hidden_step, 0)

    sent = far[0] + far[1] + near[0] + near[1] + relays[0] + relays[1] + stats[0] + stats[1] + owed
    sent += [give(2), give(3)] + [give_far(0), give_far(1)]
    for copy in sent:
        copy.wait_send()


def finish_kernel(hidden_in, dk_in, dv_in, hidden_out, dk_out, dv_out):
    hidden_out[...] = hidden_in[...]
    dk_out[...] = dk_in[...]
    dv_out[...] = dv_in[...]


def per_device(
    queries, resp_keys, resp_values, out_grad, prefix_keys, prefix_values, w_query, w_key, w_value, resp_lengths
):
    self_rows, group, size = queries.shape[1:]
    rows = self_rows * group
    half = rows // 2
    width = w_query.shape[0]
    keys = BLOCKS * SHARE
    steps = width // CHUNK // 2
    vmem, dma = pltpu.VMEM, pltpu.SemaphoreType.DMA
    whole = pl.BlockSpec(memory_space=pltpu.VMEM)
    outputs = (
        jax.ShapeDtypeStruct((self_rows // HEADS, width), BF16),
        jax.ShapeDtypeStruct((SHARE, size), BF16),
        jax.ShapeDtypeStruct((SHARE, size), BF16),
    )
    results = pl.pallas_call(
        kernel,
        out_shape=outputs,
        in_specs=[pl.BlockSpec(memory_space=pl.ANY)] * 10,
        out_specs=(whole, whole, whole),
        scratch_shapes=[
            pltpu.SMEM(resp_lengths.shape, jnp.int32),
            vmem((2, 2, rows, size), BF16),
            vmem((2, 2, rows, size), BF16),
            vmem((keys, size), BF16),
            vmem((keys, size), BF16),
            vmem((RESPS * rows, 2 * size), BF16),
            vmem((size, keys), BF16),
            vmem((keys, RESPS * rows), BF16),
            vmem((keys, RESPS * rows), BF16),
            vmem((BLOCKS, 1, RESPS * rows), F32),
            vmem((BLOCKS, 1, RESPS * rows), F32),
            vmem((BLOCKS, 1, RESPS * rows), F32),
            vmem((1, RESPS * rows), F32),
            vmem((1, RESPS * rows), F32),
            vmem((self_rows, size), BF16),
            vmem((self_rows, size), BF16),
            vmem((2, self_rows, half), BF16),
            vmem((2, self_rows, half), BF16),
            vmem((2, 3, 1, half), F32),
            vmem((2, 2 * RESPS, half), F32),
            vmem((2, RESPS, 2 * RESPS, half), F32),
            vmem((2, size, half), F32),
            vmem((2, size, rows), F32),
            vmem((4, size, half), F32),
            vmem((2, size, half), BF16),
            vmem((2, size, half), BF16),
            vmem((half, size), F32),
            vmem((self_rows, 2 * size), F32),
            vmem((2, self_rows // 2, (group + 2) * size), BF16),
            vmem((RING, CHUNK, (group + 2) * size), BF16),
            vmem((HEADS - 1, 2, steps, 2 * self_rows // HEADS, CHUNK // 2), BF16),
            vmem((keys, size), F32),
            vmem((keys, size), F32),
            vmem((BLOCKS - 1, SHARE, size), BF16),
            vmem((BLOCKS - 1, SHARE, size), BF16),
            dma((5 + 4 * HEADS,)),
            dma((RING, 3)),
            dma((2, 2)),
            dma((2, 2)),
            dma((2, 2)),
            dma((2, 2)),
            dma((2, 2)),
            dma((2, 2)),
            dma((BLOCKS,)),
            dma((BLOCKS,)),
            dma((BLOCKS,)),
            dma((BLOCKS,)),
            dma((2, RESPS)),
            dma((2, RESPS)),
            dma((4,)),
            dma((4,)),
            dma((2,)),
            dma((2,)),
            dma((BLOCKS,)),
            dma((BLOCKS,)),
            dma((BLOCKS,)),
            dma((BLOCKS,)),
            dma((2, steps, HEADS)),
            dma((2, steps, HEADS)),
        ],
        compiler_params=pltpu.CompilerParams(
            collective_id=0, has_side_effects=True, vmem_limit_bytes=65400 * 1024
        ),
    )(
        resp_lengths,
        queries.reshape(rows, size),
        out_grad.reshape(rows, size),
        resp_keys.reshape(self_rows, size),
        resp_values.reshape(self_rows, size),
        prefix_keys.reshape(SHARE, size),
        prefix_values.reshape(SHARE, size),
        w_query,
        w_key,
        w_value,
    )
    hidden, dk, dv = pl.pallas_call(
        finish_kernel, out_shape=outputs, in_specs=[whole] * 3, out_specs=(whole,) * 3
    )(*results)
    return hidden[None], dk[:, None], dv[:, None]


def solution(mesh):
    in_specs = (
        P("resp", None, "head", None),
        P("resp", None, "head", None),
        P("resp", None, "head", None),
        P("resp", None, "head", None),
        P("resp", "head", None),
        P("resp", "head", None),
        P(None, "head"),
        P(None, "head"),
        P(None, "head"),
        P(),
    )
    out_specs = (P("resp", "head", None), P("resp", "head", None), P("resp", "head", None))
    return jax.shard_map(
        per_device, mesh=mesh, in_specs=in_specs, out_specs=out_specs, check_vma=False
    )
```
